32 devices in a mesh: clip: 2 (over y), tm: 8 (over z, x), tile: 2 (over core).
Axes of the slice: x: 2, y: 2, z: 4, core: 2. Of those that a mesh axis runs over, the one named last changes fastest.
Arguments:
- queries: bfloat16 [32, 256, 2048], P(('clip', 'tm'), 'tile'), parts along dimension 0, may hold values from -48 to 48
- keyvals: bfloat16 [2, 32, 256, 512], P(None, ('clip', 'tm'), 'tile'), parts along dimension 1, may hold values from -4 to 4
- proj_weight: bfloat16 [2048, 1024], P('tm', 'tile'), may hold values from -0.125 to 0.125
- norm_gain: float32 [1024], P('tile'), may hold values from 0.25 to 1.75
- frame_counts: int32 [32], P(('clip', 'tm')), parts along dimension 0, may hold values from 129 to 256, as said below
Outputs:
- dynamics: bfloat16 [32, 256, 1024], P(('clip', 'tm'), None, 'tile'), parts along dimension 0
The draws below stay inside these ranges and needn't reach their ends.
There are 2 independent parts, one for each index of `clip`. The reference program is written for one: setup_inputs(seed, part) draws one part's arguments, and reference() takes and returns one part's arrays. A program takes and returns all parts, laid end to end along the dimension named above; an argument that names none is the same for every part. Nothing has to cross between parts.
Inputs may be any that keep to these rules, and one draw needn't show every extreme that they name: `frame_counts`: every spatial tile of every frame holds a live slot; some frame is full.
All inputs are finite; a program needn't handle non-finite values.
Results may differ from the reference program's by a relative error of at most 0.013.
Values may be sent and summed in bfloat16 or wider, within the bound.
A program may use at most 64 MiB of HBM per device.

```python
import jax
import jax.numpy as jnp
from jax import lax

FRAME_TOK = 256
QHEADS = 16
KVHEADS = 4
HEAD_DIM = 128
IDM_HEADS = 16
IDM_DIM = 64
WINDOW = 4
PARTNER = 16
QWIDTH = 2048
KVWIDTH = 512
LATENT = 1024
FRAMES = 16
TILES = 2
TILE_TOK = 128


def paired_inputs(key):
    folded = jax.random.fold_in(key, 101)
    query_key, value_key = jax.random.split(folded, 2)
    queries = jnp.clip(jax.random.normal(query_key, (FRAMES, FRAME_TOK, QWIDTH), jnp.float32), -4.0, 4.0)
    keyvals = jnp.clip(jax.random.normal(value_key, (2, FRAMES, FRAME_TOK, KVWIDTH), jnp.float32), -4.0, 4.0)
    return (queries, keyvals)


def draw_queries(key, part):
    return paired_inputs(key)[0].astype(jnp.bfloat16)


def draw_keyvals(key, part):
    return paired_inputs(key)[1].astype(jnp.bfloat16)


def draw_frame_counts(key, part):
    folded = jax.random.fold_in(key, 202)
    count_key, pick_key = jax.random.split(folded)
    lowest = FRAME_TOK - TILE_TOK + 1
    counts = jax.random.randint(count_key, (FRAMES,), lowest, FRAME_TOK + 1)
    picked = jax.random.permutation(pick_key, FRAMES)
    counts = counts.at[picked[0]].set(FRAME_TOK).at[picked[1]].set(lowest)
    return counts.astype(jnp.int32)


def level_of(stream_key, shape, cuts, low, high):
    def one(axis_at, parts):
        steps = jax.random.uniform(jax.random.fold_in(jax.random.fold_in(stream_key, 6), axis_at), (parts,), jnp.float32, low / len(cuts), high / len(cuts))
        return jnp.repeat(jnp.exp(steps), shape[axis_at] // parts).reshape((-1,) + (1,) * (len(shape) - axis_at - 1))

    loudness = one(*cuts[0])
    for cut in cuts[1:]:
        loudness = loudness * one(*cut)
    return loudness


def noise(own_key, shape, deviation, limit, pieces=(), kind=jnp.bfloat16):
    values = deviation * jax.random.normal(own_key, shape, jnp.float32)
    if pieces:
        values = values * level_of(own_key, shape, pieces, -0.22, 0.18)
    return jnp.clip(values, -limit, limit).astype(kind)


def setup_inputs(seed: int = 0, part: int = 0) -> dict:
    arg_keys = jax.random.split(jax.random.key(seed), 6)
    own_keys = jax.random.split(jax.random.fold_in(arg_keys[5], part), 6)
    return {
        "queries": draw_queries(jax.random.fold_in(jax.random.fold_in(arg_keys[5], part), 71), part),
        "keyvals": draw_keyvals(jax.random.fold_in(jax.random.fold_in(arg_keys[5], part), 71), part),
        "proj_weight": noise(arg_keys[2], (QWIDTH, LATENT), QWIDTH ** -0.5, 0.125, ((0, 8), (1, 2))),
        "norm_gain": jnp.clip(1.0 + 0.15 * jax.random.normal(arg_keys[3], (LATENT,), jnp.float32), 0.25, 1.75),
        "frame_counts": draw_frame_counts(jax.random.fold_in(jax.random.fold_in(arg_keys[5], part), 71), part),
    }


def window_attention(query_block, key_block, value_block, live_keys):
    row_count = query_block.shape[0]
    grouped = query_block.astype(jnp.float32).reshape(row_count, KVHEADS, QHEADS // KVHEADS, HEAD_DIM)
    scores = jnp.einsum('ikgd,jkd->ikgj', grouped, key_block.astype(jnp.float32)) * HEAD_DIM ** (-0.5)
    key_mask = live_keys[None, None, None, :]
    row_max = lax.optimization_barrier(jnp.max(jnp.where(key_mask, scores, -1e+30), axis=-1, keepdims=True))
    weights = jnp.where(key_mask, jnp.exp(jnp.where(key_mask, scores, row_max) - row_max), 0.0)
    normalized = (weights / lax.optimization_barrier(jnp.sum(weights, axis=-1, keepdims=True))).astype(jnp.bfloat16)
    blended = jnp.einsum('ikgj,jkd->ikgd', normalized.astype(jnp.float32), value_block.astype(jnp.float32))
    return blended.astype(jnp.bfloat16).reshape(row_count, QWIDTH)

def normalize_heads(latent_block, gain):
    width = latent_block.shape[-1]
    heads = width // IDM_DIM
    values = latent_block.astype(jnp.float32).reshape(latent_block.shape[:-1] + (heads, IDM_DIM))
    scaled = values * lax.rsqrt(lax.optimization_barrier(jnp.mean(values * values, axis=-1, keepdims=True)) + 1e-06)
    scaled = scaled * gain.astype(jnp.float32).reshape(heads, IDM_DIM)
    return scaled.astype(jnp.bfloat16).reshape(latent_block.shape)

def reference(queries, keyvals, proj_weight, norm_gain, frame_counts):
    tile_tokens = FRAME_TOK // TILES
    lead_frames = WINDOW - 1
    padded_kv = jnp.concatenate([jnp.zeros((2, lead_frames, FRAME_TOK, KVWIDTH), keyvals.dtype), keyvals], axis=1)
    padded_counts = jnp.concatenate([jnp.zeros((lead_frames,), jnp.int32), frame_counts.astype(jnp.int32)])
    slot_index = jnp.arange(FRAME_TOK, dtype=jnp.int32).reshape(TILES, tile_tokens)

    def first_section(frame_index):
        query_frame = lax.dynamic_index_in_dim(queries, frame_index, 0, keepdims=False).reshape(TILES, tile_tokens, QWIDTH)
        window_kv = lax.dynamic_slice_in_dim(padded_kv, frame_index, WINDOW, 1)
        window_counts = lax.dynamic_slice_in_dim(padded_counts, frame_index, WINDOW, 0)
        tiled_kv = window_kv.reshape(2, WINDOW, TILES, tile_tokens, KVHEADS, HEAD_DIM)
        tiled_kv = tiled_kv.transpose(0, 2, 1, 3, 4, 5).reshape(2, TILES, WINDOW * tile_tokens, KVHEADS, HEAD_DIM)
        live_keys = slot_index[None, :, :] < window_counts[:, None, None]
        live_keys = live_keys.transpose(1, 0, 2).reshape(TILES, WINDOW * tile_tokens)
        result = jax.vmap(window_attention)(query_frame, tiled_kv[0], tiled_kv[1], live_keys)
        return result.reshape(FRAME_TOK, QWIDTH)
    attended = lax.map(first_section, jnp.arange(FRAMES, dtype=jnp.int32))
    latent = jnp.dot(attended.reshape(FRAMES * FRAME_TOK, QWIDTH), proj_weight, preferred_element_type=jnp.float32)
    latent = latent.astype(jnp.bfloat16).reshape(FRAMES, FRAME_TOK, LATENT)
    normed = normalize_heads(latent, norm_gain)
    blank_frames = jnp.zeros((PARTNER, FRAME_TOK, LATENT), jnp.bfloat16)
    padded_normed = jnp.concatenate([blank_frames, normed, blank_frames], axis=0)
    blank_counts = jnp.zeros((PARTNER,), jnp.int32)
    padded_live = jnp.concatenate([blank_counts, frame_counts.astype(jnp.int32), blank_counts])
    slot_all = jnp.arange(FRAME_TOK, dtype=jnp.int32)

    def second_section(frame_index):
        key_frames = []
        live_parts = []
        for offset_frames in (0, PARTNER, 2 * PARTNER):
            key_frames.append(lax.dynamic_index_in_dim(padded_normed, frame_index + offset_frames, 0, keepdims=False))
            count_here = lax.dynamic_index_in_dim(padded_live, frame_index + offset_frames, 0, keepdims=False)
            live_parts.append(slot_all < count_here)
        key_rows = jnp.concatenate(key_frames, axis=0).reshape(3 * FRAME_TOK, IDM_HEADS, IDM_DIM).astype(jnp.float32)
        live_keys = jnp.concatenate(live_parts)
        query_rows = key_frames[1].reshape(FRAME_TOK, IDM_HEADS, IDM_DIM).astype(jnp.float32)
        scores = jnp.einsum('ihd,jhd->ihj', query_rows, key_rows) * IDM_DIM ** (-0.5)
        weights = jnp.where(live_keys[None, None, :], jnp.exp(scores), 0.0)
        normalized = (weights / lax.optimization_barrier(jnp.sum(weights, axis=-1, keepdims=True))).astype(jnp.bfloat16)
        blended = jnp.einsum('ihj,jhd->ihd', normalized.astype(jnp.float32), key_rows)
        return blended.astype(jnp.bfloat16).reshape(FRAME_TOK, LATENT)
    return lax.map(second_section, jnp.arange(FRAMES, dtype=jnp.int32))
```

```python
import functools
import math

import jax
import jax.numpy as jnp
from jax import lax
from jax.experimental import pallas as pl
from jax.experimental.pallas import tpu as pltpu
from jax.sharding import PartitionSpec as P

QHEADS = 16
KVHEADS = 4
HEAD_DIM = 128
IDM_DIM = 64
WINDOW = 4
PARTNER = 16
LEAD = WINDOW - 1
LANES = 128
TILE_ROWS = 16
DEAD = -1e30
LOG2E = math.log2(math.e)
MESH = pl.DeviceIdType.MESH


def passed_along(value, axis, steps):
    count = lax.axis_size(axis)
    initial, last = (max(0, -steps), min(count, count - steps))
    return lax.ppermute(value, axis, [(source, source + steps) for source in range(initial, last)])


def columns_of(mesh):
    place = mesh.axis_names.index("tm")
    line = mesh.devices.transpose(
        [place] + [i for i in range(mesh.devices.ndim) if i != place]
    ).reshape(mesh.shape["tm"], -1)[:, 0]
    coords = [getattr(device, "coords", None) for device in line]
    if coords[0] is None or len(line) == 1:
        return 1
    moved = [i for i in range(len(coords[0])) if coords[0][i] != coords[1][i]]
    if len(moved) != 1:
        return 1
    columns = len({c[moved[0]] for c in coords})
    return columns if len(line) % columns == 0 else 1


def halo_plan(frames):
    plan, covered, hop = [], 0, 1
    while covered < LEAD:
        needed = min(frames, LEAD - covered)
        covered += needed
        plan.append((hop, needed, LEAD - covered))
        hop += 1
    return plan


def ring_chunks(rows, clip, clips):
    third = (rows // TILE_ROWS // 3) * TILE_ROWS if clips == 2 else 0
    chunks = []
    if third:
        chunks.append((clip * (rows - third), third, True))
    chunks.append((third, rows - 2 * third, False))
    return chunks


def latent_kernel(
    n, clips, tiles, x_count,
    counts_ref, q_ref, kv_ref, w_ref, gain_ref, out_ref,
    q_buf, kv_win, w_full, att, counts, bias,
    local_sem, halo_send, halo_recv, count_send, count_recv,
    ring_send, ring_recv, clip_send, clip_recv, tile_send, tile_recv,
):
    clip, tm, tile = lax.axis_index("clip"), lax.axis_index("tm"), lax.axis_index("tile")
    frames, tokens, width = q_ref.shape
    rows = w_ref.shape[0]
    groups = QHEADS // KVHEADS
    plan = halo_plan(frames)
    z_count = n // x_count

    def place_of(index):
        x, z = lax.rem(index, x_count), index // x_count
        return x * z_count + z + lax.rem(x, 2) * (z_count - 1 - 2 * z)

    def index_of(place):
        place = lax.rem(place + 2 * n, n)
        x, z = place // z_count, lax.rem(place, z_count)
        return (z + lax.rem(x, 2) * (z_count - 1 - 2 * z)) * x_count + x

    place = place_of(tm)
    ends = (index_of(place + 1), index_of(place - 1))

    own_copies = [
        pltpu.make_async_copy(kv_ref, kv_win.at[:, LEAD:LEAD + frames], local_sem.at[0]),
        pltpu.make_async_copy(q_ref, q_buf, local_sem.at[1]),
        pltpu.make_async_copy(w_ref, w_full.at[tm], local_sem.at[2]),
    ]
    for copy in own_copies:
        copy.start()

    barrier = pltpu.get_barrier_semaphore()
    expected = 0
    if n > 1:
        for end in ends:
            pl.semaphore_signal(barrier, inc=1, device_id={"tm": end}, device_id_type=MESH)
            expected += 1
    if clips == 2:
        pl.semaphore_signal(barrier, inc=1, device_id={"clip": 1 - clip}, device_id_type=MESH)
        expected += 1
    if tiles == 2:
        pl.semaphore_signal(barrier, inc=1, device_id={"tile": 1 - tile}, device_id_type=MESH)
        expected += 1
    for hop, _, _ in plan:
        @pl.when(tm + hop < n)
        def _():
            pl.semaphore_signal(barrier, inc=1, device_id={"tm": tm + hop}, device_id_type=MESH)

        @pl.when(tm >= hop)
        def _():
            pl.semaphore_signal(barrier, inc=1, device_id={"tm": tm - hop}, device_id_type=MESH)

        expected = expected + jnp.where(tm + hop < n, 1, 0) + jnp.where(tm >= hop, 1, 0)
    for f in range(frames):
        counts[0, f:f + 1, :] = jnp.full((1, LANES), counts_ref[f], jnp.int32)
    pl.semaphore_wait(barrier, expected)

    halo = []
    for i, (hop, needed, start) in enumerate(plan):
        target = {"tm": lax.rem(tm + hop, n)}
        halo.append((
            hop,
            pltpu.make_async_remote_copy(
                src_ref=kv_ref.at[:, frames - needed:frames],
                dst_ref=kv_win.at[:, start:start + needed],
                send_sem=halo_send.at[i], recv_sem=halo_recv.at[i],
                device_id=target, device_id_type=MESH),
            pltpu.make_async_remote_copy(
                src_ref=counts.at[0], dst_ref=counts.at[hop],
                send_sem=count_send.at[i], recv_sem=count_recv.at[i],
                device_id=target, device_id_type=MESH),
        ))
    for hop, kv_copy, count_copy in halo:
        @pl.when(tm + hop < n)
        def _():
            count_copy.start()
            kv_copy.start()

    chunks = ring_chunks(rows, clip, clips)
    steps = n // 2
    started, later = [], []

    def ring_copy(way, step, c):
        start, size, _ = chunks[c]
        owner = index_of(place - step * (1 - 2 * way))
        span = pl.ds(start if isinstance(start, int) else pl.multiple_of(start, TILE_ROWS), size)
        slot = (way * max(steps, 1) + step) * len(chunks) + c
        return pltpu.make_async_remote_copy(
            src_ref=w_ref.at[span] if step == 0 else w_full.at[owner, span],
            dst_ref=w_full.at[owner, span],
            send_sem=ring_send.at[slot], recv_sem=ring_recv.at[slot],
            device_id={"tm": ends[way]}, device_id_type=MESH)

    def goes(way, step, c):
        return n % 2 == 1 or step < steps - 1 or c % 2 == way

    def send_step(way, step, c):
        if step < steps and goes(way, step, c):
            copy = ring_copy(way, step, c)
            copy.start()
            started.append(copy)

    def take_step(step):
        for c in range(len(chunks)):
            for way in range(2):
                if not goes(way, step, c):
                    continue
                ring_copy(way, step, c).wait_recv()
                send_step(way, step + 1, c)
                start, size, over = chunks[c]
                if over:
                    owner = index_of(place - (step + 1) * (1 - 2 * way))
                    span = pl.ds(pl.multiple_of(start, TILE_ROWS), size)
                    slot = way * max(steps, 1) + step
                    copy = pltpu.make_async_remote_copy(
                        src_ref=w_full.at[owner, span], dst_ref=w_full.at[owner, span],
                        send_sem=clip_send.at[slot], recv_sem=clip_recv.at[slot],
                        device_id={"clip": 1 - clip}, device_id_type=MESH)
                    copy.start()
                    later.append(copy)

    if steps:
        for c in range(len(chunks)):
            for way in range(2):
                send_step(way, 0, c)

    for hop, kv_copy, count_copy in halo:
        _, needed, start = plan[hop - 1]

        @pl.when(tm < hop)
        def _():
            counts[hop] = jnp.zeros(counts.shape[1:], jnp.int32)
            kv_win[:, start:start + needed] = jnp.zeros(
                (2, needed) + kv_win.shape[2:], kv_win.dtype)

    taken = 0
    if steps > 1:
        take_step(0)
        taken = 1

    for hop, kv_copy, count_copy in halo:
        @pl.when(tm >= hop)
        def _():
            count_copy.wait_recv()
            kv_copy.wait_recv()
    own_copies[0].wait()
    own_copies[1].wait()

    slots = tile * tokens + lax.broadcasted_iota(jnp.int32, (tokens, LANES), 0)
    first_lane = lax.broadcasted_iota(jnp.int32, (tokens, LANES), 1) == 0
    for w in range(LEAD + frames):
        if w >= LEAD:
            row = counts[0, w - LEAD:w - LEAD + 1, :]
        else:
            hop, needed, start = [p for p in plan if p[2] <= w < p[2] + p[1]][0]
            at = frames - needed + w - start
            row = counts[hop, at:at + 1, :]
        bias[w] = jnp.where(
            jnp.logical_and(first_lane, slots >= row), DEAD, 0.0).astype(bias.dtype)

    keys = WINDOW * tokens
    unit_lane = (
        lax.broadcasted_iota(jnp.int32, (groups * tokens, LANES), 1) == 0
    ).astype(jnp.bfloat16)
    ones = jnp.ones((keys, LANES), jnp.bfloat16)
    scale = HEAD_DIM ** (-0.5) * LOG2E
    exchanged = []
    units = frames * KVHEADS
    every = max(1, units // max(1, steps))
    for unit in range(units):
        f, g = unit // KVHEADS, unit % KVHEADS
        span = slice(g * HEAD_DIM, (g + 1) * HEAD_DIM)
        k = kv_win[0, f:f + WINDOW, :, span].reshape(keys, HEAD_DIM)
        v = kv_win[1, f:f + WINDOW, :, span].reshape(keys, HEAD_DIM)
        k = jnp.concatenate([k, bias[f:f + WINDOW].reshape(keys, LANES)], axis=1)
        v = jnp.concatenate([v, ones], axis=1)
        q = jnp.concatenate(
            [q_buf[f, :, (g * groups + i) * HEAD_DIM:(g * groups + i + 1) * HEAD_DIM]
             for i in range(groups)], axis=0)
        q = jnp.concatenate([q, unit_lane], axis=1)
        scores = lax.dot_general(q, k, (((1,), (1,)), ((), ())), preferred_element_type=jnp.float32)
        top = jnp.max(scores, axis=-1, keepdims=True)
        weights = jnp.exp2((scores - top) * scale).astype(jnp.bfloat16)
        mixed = jnp.dot(weights, v, preferred_element_type=jnp.float32)
        result = (mixed[:, :HEAD_DIM] / mixed[:, HEAD_DIM:]).astype(jnp.bfloat16)
        for i in range(groups):
            at = (g * groups + i) * HEAD_DIM
            att[f, tile, :, at:at + HEAD_DIM] = result[i * tokens:(i + 1) * tokens]
        if tiles == 2:
            part = att.at[f, tile, :, g * groups * HEAD_DIM:(g + 1) * groups * HEAD_DIM]
            copy = pltpu.make_async_remote_copy(
                src_ref=part, dst_ref=part,
                send_sem=tile_send.at[unit], recv_sem=tile_recv.at[unit],
                device_id={"tile": 1 - tile}, device_id_type=MESH)
            copy.start()
            exchanged.append(copy)
        if unit % every == every - 1 and taken < steps - 1:
            take_step(taken)
            taken += 1
    while taken < steps:
        take_step(taken)
        taken += 1

    own_copies[2].wait()
    for copy in exchanged:
        copy.wait_recv()
    for copy in later:
        copy.wait_recv()

    columns = w_ref.shape[1]
    same = (
        lax.rem(lax.broadcasted_iota(jnp.int32, (2 * LANES, LANES), 0), LANES) // IDM_DIM
        == lax.broadcasted_iota(jnp.int32, (2 * LANES, LANES), 1) // IDM_DIM
    ).astype(jnp.bfloat16)
    weight = w_full[...].reshape(n * rows, columns)
    for f in range(frames):
        token_rows = att[f].reshape(tiles * tokens, width)
        latent = jnp.dot(token_rows, weight, preferred_element_type=jnp.float32)
        latent = latent.astype(jnp.bfloat16).astype(jnp.float32)
        for c in range(0, columns, LANES):
            value = latent[:, c:c + LANES]
            square = value * value
            high = square.astype(jnp.bfloat16)
            low = (square - high.astype(jnp.float32)).astype(jnp.bfloat16)
            total = jnp.dot(
                jnp.concatenate([high, low], axis=1), same, preferred_element_type=jnp.float32)
            scaled = value * lax.rsqrt(total * (1.0 / IDM_DIM) + 1e-6) * gain_ref[:, c:c + LANES]
            out_ref[f, :, c:c + LANES] = scaled.astype(out_ref.dtype)

    for copy in started + later + exchanged:
        copy.wait_send()
    for hop, kv_copy, count_copy in halo:
        @pl.when(tm + hop < n)
        def _():
            count_copy.wait_send()
            kv_copy.wait_send()


def normed_latent(mesh, queries, keyvals, proj_weight, norm_gain, frame_counts):
    n, clips, tiles = (mesh.shape[a] for a in ("tm", "clip", "tile"))
    frames, tokens, width = queries.shape
    rows, columns = proj_weight.shape
    hops = len(halo_plan(frames))
    steps = max(1, n // 2)
    units = frames * KVHEADS
    dma = pltpu.SemaphoreType.DMA
    any_spec = pl.BlockSpec(memory_space=pl.ANY)
    vmem = pl.BlockSpec(memory_space=pltpu.VMEM)
    bf16 = jnp.bfloat16
    flops = frames * tokens * width * 4 * WINDOW * tokens + 2 * frames * tiles * tokens * width * columns
    return pl.pallas_call(
        functools.partial(latent_kernel, n, clips, tiles, columns_of(mesh)),
        out_shape=jax.ShapeDtypeStruct((frames, tiles * tokens, columns), bf16),
        in_specs=[pl.BlockSpec(memory_space=pltpu.SMEM), any_spec, any_spec, any_spec, vmem],
        out_specs=vmem,
        scratch_shapes=[
            pltpu.VMEM(queries.shape, bf16),
            pltpu.VMEM((2, LEAD + frames) + keyvals.shape[2:], bf16),
            pltpu.VMEM((n, rows, columns), bf16),
            pltpu.VMEM((frames, tiles, tokens, width), bf16),
            pltpu.VMEM((hops + 1, max(8, frames), LANES), jnp.int32),
            pltpu.VMEM((LEAD + frames, tokens, LANES), bf16),
            dma((3,)), dma((hops,)), dma((hops,)), dma((hops,)), dma((hops,)),
            dma((4 * steps,)), dma((4 * steps,)), dma((2 * steps,)), dma((2 * steps,)),
            dma((units,)), dma((units,)),
        ],
        compiler_params=pltpu.CompilerParams(
            collective_id=0, has_side_effects=True, vmem_limit_bytes=48 * 2 ** 20),
        cost_estimate=pl.CostEstimate(
            flops=flops, bytes_accessed=8 * 2 ** 20, transcendentals=0),
    )(frame_counts, queries, keyvals, proj_weight, norm_gain.reshape(1, -1))


def partner_kernel(sources, counts_ref, *refs):
    out_ref = refs[-1]
    frame = pl.program_id(0)
    tokens, columns = out_ref.shape[1:]
    keys = sources * tokens
    slots = lax.broadcasted_iota(jnp.int32, (tokens, LANES), 0)
    live = jnp.concatenate(
        [slots < counts_ref[source, frame] for source in range(sources)], axis=0)
    lower = lax.broadcasted_iota(jnp.int32, (tokens, LANES), 1) < IDM_DIM
    scale = IDM_DIM ** (-0.5) * LOG2E
    for c in range(0, columns, LANES):
        k = jnp.concatenate([ref[0, :, c:c + LANES] for ref in refs[:sources]], axis=0)
        q = refs[0][0, :, c:c + LANES]
        zero = jnp.zeros_like(q)
        q = jnp.concatenate([jnp.where(lower, q, zero), jnp.where(lower, zero, q)], axis=0)
        v = jnp.concatenate(
            [jnp.where(live, k, jnp.zeros_like(k)), live.astype(k.dtype)], axis=1)
        scores = lax.dot_general(q, k, (((1,), (1,)), ((), ())), preferred_element_type=jnp.float32)
        weights = jnp.exp2(scores * scale).astype(jnp.bfloat16)
        mixed = jnp.dot(weights, v, preferred_element_type=jnp.float32)
        result = mixed[:, :LANES] / mixed[:, LANES:]
        out_ref[0, :, c:c + LANES] = jnp.where(
            lower, result[:tokens], result[tokens:]).astype(out_ref.dtype)


def partner_attention(counts, blocks):
    frames, tokens, columns = blocks[0].shape
    spec = pl.BlockSpec((1, tokens, columns), lambda f: (f, 0, 0))
    return pl.pallas_call(
        functools.partial(partner_kernel, len(blocks)),
        out_shape=jax.ShapeDtypeStruct(blocks[0].shape, jnp.bfloat16),
        grid=(frames,),
        in_specs=[pl.BlockSpec(memory_space=pltpu.SMEM)] + [spec] * len(blocks),
        out_specs=spec,
        compiler_params=pltpu.CompilerParams(vmem_limit_bytes=32 * 2 ** 20),
    )(counts, *blocks)


def local(mesh, queries, keyvals, proj_weight, norm_gain, frame_counts):
    normed = normed_latent(mesh, queries, keyvals, proj_weight, norm_gain, frame_counts)
    distance = PARTNER // queries.shape[0]
    blocks, counts = [normed], [frame_counts]
    for steps in (distance, -distance):
        if distance < mesh.shape["tm"]:
            block, count = passed_along((normed, frame_counts), "tm", steps)
            blocks.append(block)
            counts.append(count)
    return partner_attention(jnp.stack(counts), blocks)


def solution(mesh):
    in_specs = (
        P(("clip", "tm"), "tile", None),
        P(None, ("clip", "tm"), "tile", None),
        P("tm", "tile"),
        P("tile"),
        P(("clip", "tm")),
    )
    out_specs = P(("clip", "tm"), None, "tile")
    return jax.shard_map(
        functools.partial(local, mesh), mesh=mesh, in_specs=in_specs, out_specs=out_specs,
        check_vma=False)
```

```python
import functools
import math

import jax
import jax.numpy as jnp
from jax import lax
from jax.experimental import pallas as pl
from jax.experimental.pallas import tpu as pltpu
from jax.sharding import PartitionSpec as P

QHEADS = 16
KVHEADS = 4
HEAD_DIM = 128
IDM_DIM = 64
WINDOW = 4
PARTNER = 16
LEAD = WINDOW - 1
LANES = 128
TILE_ROWS = 16
DEAD = -1e30
LOG2E = math.log2(math.e)
MESH = pl.DeviceIdType.MESH


def passed_along(value, axis, steps):
    count = lax.axis_size(axis)
    initial, last = (max(0, -steps), min(count, count - steps))
    return lax.ppermute(value, axis, [(source, source + steps) for source in range(initial, last)])


def columns_of(mesh):
    place = mesh.axis_names.index("tm")
    line = mesh.devices.transpose(
        [place] + [i for i in range(mesh.devices.ndim) if i != place]
    ).reshape(mesh.shape["tm"], -1)[:, 0]
    coords = [getattr(device, "coords", None) for device in line]
    if coords[0] is None or len(line) == 1:
        return 1
    moved = [i for i in range(len(coords[0])) if coords[0][i] != coords[1][i]]
    if len(moved) != 1:
        return 1
    columns = len({c[moved[0]] for c in coords})
    return columns if len(line) % columns == 0 else 1


def halo_plan(frames):
    plan, covered, hop = [], 0, 1
    while covered < LEAD:
        needed = min(frames, LEAD - covered)
        covered += needed
        plan.append((hop, needed, LEAD - covered))
        hop += 1
    return plan


def relayed(plan, x_count, n):
    return x_count == 2 and n % 2 == 0 and len(plan) == 2 and plan[0][1] > plan[1][1]


def ring_chunks(rows, clip, clips):
    over = clips == 2 and rows % (2 * TILE_ROWS) == 0
    start, size = (clip * (rows // 2), rows // 2) if over else (0, rows)
    if size % (2 * TILE_ROWS):
        return [(start, size, over)]
    return [(start, size // 2, over), (start + size // 2, size // 2, over)]


def latent_kernel(
    n, clips, tiles, x_count,
    counts_ref, q_ref, kv_ref, w_ref, gain_ref, out_ref,
    q_buf, kv_win, stash, w_full, att, counts, bias,
    local_sem, halo_send, halo_recv, count_send, count_recv,
    ring_send, ring_recv, clip_send, clip_recv, tile_send, tile_recv,
):
    clip, tm, tile = lax.axis_index("clip"), lax.axis_index("tm"), lax.axis_index("tile")
    frames, tokens, width = q_ref.shape
    rows = w_ref.shape[0]
    groups = QHEADS // KVHEADS
    plan = halo_plan(frames)
    z_count = n // x_count

    def place_of(index):
        x, z = lax.rem(index, x_count), index // x_count
        return x * z_count + z + lax.rem(x, 2) * (z_count - 1 - 2 * z)

    def index_of(place):
        place = lax.rem(place + 2 * n, n)
        x, z = place // z_count, lax.rem(place, z_count)
        return (z + lax.rem(x, 2) * (z_count - 1 - 2 * z)) * x_count + x

    place = place_of(tm)
    ends = (index_of(place + 1), index_of(place - 1))

    own_copies = [
        pltpu.make_async_copy(kv_ref, kv_win.at[:, LEAD:LEAD + frames], local_sem.at[0]),
        pltpu.make_async_copy(q_ref, q_buf, local_sem.at[1]),
        pltpu.make_async_copy(w_ref, w_full.at[tm], local_sem.at[2]),
    ]
    for copy in own_copies:
        copy.start()

    barrier = pltpu.get_barrier_semaphore()
    expected = 0
    if n > 1:
        for end in ends:
            pl.semaphore_signal(barrier, inc=1, device_id={"tm": end}, device_id_type=MESH)
            expected += 1
    if clips == 2:
        pl.semaphore_signal(barrier, inc=1, device_id={"clip": 1 - clip}, device_id_type=MESH)
        expected += 1
    if tiles == 2:
        pl.semaphore_signal(barrier, inc=1, device_id={"tile": 1 - tile}, device_id_type=MESH)
        expected += 1
    for hop, _, _ in plan:
        @pl.when(tm + hop < n)
        def _():
            pl.semaphore_signal(barrier, inc=1, device_id={"tm": tm + hop}, device_id_type=MESH)

        @pl.when(tm >= hop)
        def _():
            pl.semaphore_signal(barrier, inc=1, device_id={"tm": tm - hop}, device_id_type=MESH)

        expected = expected + jnp.where(tm + hop < n, 1, 0) + jnp.where(tm >= hop, 1, 0)
    for f in range(frames):
        counts[0, f:f + 1, :] = jnp.full((1, LANES), counts_ref[f], jnp.int32)
    pl.semaphore_wait(barrier, expected)

    count_copies = []
    for i, (hop, _, _) in enumerate(plan):
        count_copies.append((hop, pltpu.make_async_remote_copy(
            src_ref=counts.at[0], dst_ref=counts.at[hop],
            send_sem=count_send.at[i], recv_sem=count_recv.at[i],
            device_id={"tm": lax.rem(tm + hop, n)}, device_id_type=MESH)))
    for hop, copy in count_copies:
        pl.when(tm + hop < n)(copy.start)

    def halo_copy(role, arrival, g, source, first, count, place_at, hop):
        span = pl.ds(g * HEAD_DIM, HEAD_DIM)
        target = stash if place_at is None else kv_win.at[:, place_at:place_at + count]
        return pltpu.make_async_remote_copy(
            src_ref=source.at[:, first:first + count, :, span],
            dst_ref=target.at[:, :, :, span],
            send_sem=halo_send.at[role * KVHEADS + g],
            recv_sem=halo_recv.at[arrival * KVHEADS + g],
            device_id={"tm": lax.rem(tm + hop + n, n)}, device_id_type=MESH)

    firsts, relays, arrivals = [], [], []
    if relayed(plan, x_count, n):
        (_, needed, start), (_, last, start2) = plan
        rest = needed - last
        even, odd = lax.rem(tm, 2) == 0, lax.rem(tm, 2) == 1
        up, down = tm + 2 < n, tm >= 2
        for g in range(KVHEADS):
            firsts += [
                (halo_copy(2, 2, g, kv_ref, frames - last, last, start2, 2), up),
                (halo_copy(3, 3, g, kv_ref, frames - needed, rest, None, -1),
                 jnp.logical_and(odd, up)),
                (halo_copy(0, 0, g, kv_ref, frames - needed, rest, start, 1), even),
                (halo_copy(1, 1, g, kv_ref, frames - last, last, start + rest, 1), even),
            ]
            relays.append([
                (halo_copy(4, 0, g, stash, 0, rest, start, 2), jnp.logical_and(even, up), 3),
                (halo_copy(5, 1, g, kv_win, start2, last, start + rest, -1),
                 jnp.logical_and(odd, down), 2),
            ])
            arrivals.append([
                (0, tm >= 1, rest, start), (1, tm >= 1, last, start + rest),
                (2, jnp.logical_and(even, down), last, start2),
            ])
    else:
        for g in range(KVHEADS):
            for i, (hop, needed, start) in enumerate(plan):
                firsts.append((
                    halo_copy(i, i, g, kv_ref, frames - needed, needed, start, hop), tm + hop < n))
            relays.append([])
            arrivals.append([
                (i, tm >= hop, needed, start) for i, (hop, needed, start) in enumerate(plan)])
    for copy, mine in firsts:
        pl.when(mine)(copy.start)

    def arrival_of(arrival, g, count, place_at):
        return halo_copy(0, arrival, g, kv_ref, 0, count, place_at, 1)

    def relay(g):
        for copy, mine, arrival in relays[g]:
            @pl.when(mine)
            def _():
                count, place_at = (rest, None) if arrival == 3 else (last, start2)
                arrival_of(arrival, g, count, place_at).wait_recv()
                copy.start()

    def arrive(g):
        for arrival, mine, count, place_at in arrivals[g]:
            pl.when(mine)(arrival_of(arrival, g, count, place_at).wait_recv)

    chunks = ring_chunks(rows, clip, clips)
    steps = n // 2
    started, later = [], []

    def ring_copy(way, step, c):
        start, size, _ = chunks[c]
        owner = index_of(place - step * (1 - 2 * way))
        span = pl.ds(start if isinstance(start, int) else pl.multiple_of(start, TILE_ROWS), size)
        slot = (way * max(steps, 1) + step) * len(chunks) + c
        return pltpu.make_async_remote_copy(
            src_ref=w_ref.at[span] if step == 0 else w_full.at[owner, span],
            dst_ref=w_full.at[owner, span],
            send_sem=ring_send.at[slot], recv_sem=ring_recv.at[slot],
            device_id={"tm": ends[way]}, device_id_type=MESH)

    def goes(way, step, c):
        return n % 2 == 1 or step < steps - 1 or c % 2 == way

    def send_step(way, step, c):
        if step < steps and goes(way, step, c):
            copy = ring_copy(way, step, c)
            copy.start()
            started.append(copy)

    def take_step(step):
        for c in range(len(chunks)):
            for way in range(2):
                if not goes(way, step, c):
                    continue
                ring_copy(way, step, c).wait_recv()
                send_step(way, step + 1, c)
                start, size, over = chunks[c]
                if over:
                    owner = index_of(place - (step + 1) * (1 - 2 * way))
                    span = pl.ds(pl.multiple_of(start, TILE_ROWS), size)
                    slot = (way * steps + step) * len(chunks) + c
                    copy = pltpu.make_async_remote_copy(
                        src_ref=w_full.at[owner, span], dst_ref=w_full.at[owner, span],
                        send_sem=clip_send.at[slot], recv_sem=clip_recv.at[slot],
                        device_id={"clip": 1 - clip}, device_id_type=MESH)
                    copy.start()
                    later.append(copy)

    if steps:
        for c in range(len(chunks)):
            for way in range(2):
                send_step(way, 0, c)

    for hop, needed, start in plan:
        @pl.when(tm < hop)
        def _():
            counts[hop] = jnp.zeros(counts.shape[1:], jnp.int32)
            kv_win[:, start:start + needed] = jnp.zeros(
                (2, needed) + kv_win.shape[2:], kv_win.dtype)

    for hop, copy in count_copies:
        pl.when(tm >= hop)(copy.wait_recv)
    own_copies[0].wait()
    own_copies[1].wait()

    slots = tile * tokens + lax.broadcasted_iota(jnp.int32, (tokens, LANES), 0)
    first_lane = lax.broadcasted_iota(jnp.int32, (tokens, LANES), 1) == 0
    for w in range(LEAD + frames):
        if w >= LEAD:
            row = counts[0, w - LEAD:w - LEAD + 1, :]
        else:
            hop, needed, start = [p for p in plan if p[2] <= w < p[2] + p[1]][0]
            at = frames - needed + w - start
            row = counts[hop, at:at + 1, :]
        bias[w] = jnp.where(
            jnp.logical_and(first_lane, slots >= row), DEAD, 0.0).astype(bias.dtype)

    keys = WINDOW * tokens
    unit_lane = (
        lax.broadcasted_iota(jnp.int32, (groups * tokens, LANES), 1) == 0
    ).astype(jnp.bfloat16)
    ones = jnp.ones((keys, LANES), jnp.bfloat16)
    scale = HEAD_DIM ** (-0.5) * LOG2E
    exchanged = []
    taken = 0
    relay(0)
    for unit in range(KVHEADS * frames):
        g, f = unit // frames, unit % frames
        if f == 0:
            if taken < steps - 1:
                take_step(taken)
                taken += 1
            if g + 1 < KVHEADS:
                relay(g + 1)
            arrive(g)
        span = slice(g * HEAD_DIM, (g + 1) * HEAD_DIM)
        k = kv_win[0, f:f + WINDOW, :, span].reshape(keys, HEAD_DIM)
        v = kv_win[1, f:f + WINDOW, :, span].reshape(keys, HEAD_DIM)
        k = jnp.concatenate([k, bias[f:f + WINDOW].reshape(keys, LANES)], axis=1)
        v = jnp.concatenate([v, ones], axis=1)
        q = jnp.concatenate(
            [q_buf[f, :, (g * groups + i) * HEAD_DIM:(g * groups + i + 1) * HEAD_DIM]
             for i in range(groups)], axis=0)
        q = jnp.concatenate([q, unit_lane], axis=1)
        scores = lax.dot_general(q, k, (((1,), (1,)), ((), ())), preferred_element_type=jnp.float32)
        top = jnp.max(scores, axis=-1, keepdims=True)
        weights = jnp.exp2((scores - top) * scale).astype(jnp.bfloat16)
        mixed = jnp.dot(weights, v, preferred_element_type=jnp.float32)
        result = (mixed[:, :HEAD_DIM] / mixed[:, HEAD_DIM:]).astype(jnp.bfloat16)
        for i in range(groups):
            at = (g * groups + i) * HEAD_DIM
            att[f, tile, :, at:at + HEAD_DIM] = result[i * tokens:(i + 1) * tokens]
        if tiles == 2:
            part = att.at[f, tile, :, g * groups * HEAD_DIM:(g + 1) * groups * HEAD_DIM]
            copy = pltpu.make_async_remote_copy(
                src_ref=part, dst_ref=part,
                send_sem=tile_send.at[unit], recv_sem=tile_recv.at[unit],
                device_id={"tile": 1 - tile}, device_id_type=MESH)
            copy.start()
            exchanged.append(copy)
    while taken < steps:
        take_step(taken)
        taken += 1

    own_copies[2].wait()
    for copy in exchanged:
        copy.wait_recv()
    for copy in later:
        copy.wait_recv()

    columns = w_ref.shape[1]
    same = (
        lax.rem(lax.broadcasted_iota(jnp.int32, (2 * LANES, LANES), 0), LANES) // IDM_DIM
        == lax.broadcasted_iota(jnp.int32, (2 * LANES, LANES), 1) // IDM_DIM
    ).astype(jnp.bfloat16)
    weight = w_full[...].reshape(n * rows, columns)
    for f in range(frames):
        token_rows = att[f].reshape(tiles * tokens, width)
        latent = jnp.dot(token_rows, weight, preferred_element_type=jnp.float32)
        latent = latent.astype(jnp.bfloat16).astype(jnp.float32)
        for c in range(0, columns, LANES):
            value = latent[:, c:c + LANES]
            square = value * value
            high = square.astype(jnp.bfloat16)
            low = (square - high.astype(jnp.float32)).astype(jnp.bfloat16)
            total = jnp.dot(
                jnp.concatenate([high, low], axis=1), same, preferred_element_type=jnp.float32)
            scaled = value * lax.rsqrt(total * (1.0 / IDM_DIM) + 1e-6) * gain_ref[:, c:c + LANES]
            out_ref[f, :, c:c + LANES] = scaled.astype(out_ref.dtype)

    for copy in started + later + exchanged:
        copy.wait_send()
    for hop, copy in count_copies:
        pl.when(tm + hop < n)(copy.wait_send)
    for copy, mine in firsts + [entry[:2] for group in relays for entry in group]:
        pl.when(mine)(copy.wait_send)


def normed_latent(mesh, queries, keyvals, proj_weight, norm_gain, frame_counts):
    n, clips, tiles = (mesh.shape[a] for a in ("tm", "clip", "tile"))
    frames, tokens, width = queries.shape
    rows, columns = proj_weight.shape
    plan = halo_plan(frames)
    hops = len(plan)
    rest = max(1, plan[0][1] - plan[1][1]) if hops > 1 else 1
    roles = max(6, hops) * KVHEADS
    steps = max(1, n // 2)
    units = frames * KVHEADS
    dma = pltpu.SemaphoreType.DMA
    any_spec = pl.BlockSpec(memory_space=pl.ANY)
    vmem = pl.BlockSpec(memory_space=pltpu.VMEM)
    bf16 = jnp.bfloat16
    flops = frames * tokens * width * 4 * WINDOW * tokens + 2 * frames * tiles * tokens * width * columns
    return pl.pallas_call(
        functools.partial(latent_kernel, n, clips, tiles, columns_of(mesh)),
        out_shape=jax.ShapeDtypeStruct((frames, tiles * tokens, columns), bf16),
        in_specs=[pl.BlockSpec(memory_space=pltpu.SMEM), any_spec, any_spec, any_spec, vmem],
        out_specs=vmem,
        scratch_shapes=[
            pltpu.VMEM(queries.shape, bf16),
            pltpu.VMEM((2, LEAD + frames) + keyvals.shape[2:], bf16),
            pltpu.VMEM((2, rest) + keyvals.shape[2:], bf16),
            pltpu.VMEM((n, rows, columns), bf16),
            pltpu.VMEM((frames, tiles, tokens, width), bf16),
            pltpu.VMEM((hops + 1, max(8, frames), LANES), jnp.int32),
            pltpu.VMEM((LEAD + frames, tokens, LANES), bf16),
            dma((3,)), dma((roles,)), dma((roles,)), dma((hops,)), dma((hops,)),
            dma((4 * steps,)), dma((4 * steps,)), dma((4 * steps,)), dma((4 * steps,)),
            dma((units,)), dma((units,)),
        ],
        compiler_params=pltpu.CompilerParams(
            collective_id=0, has_side_effects=True, vmem_limit_bytes=60 * 2 ** 20),
        cost_estimate=pl.CostEstimate(
            flops=flops, bytes_accessed=8 * 2 ** 20, transcendentals=0),
    )(frame_counts, queries, keyvals, proj_weight, norm_gain.reshape(1, -1))


def partner_kernel(sources, counts_ref, *refs):
    out_ref = refs[-1]
    frame = pl.program_id(0)
    tokens, columns = out_ref.shape[1:]
    keys = sources * tokens
    slots = lax.broadcasted_iota(jnp.int32, (tokens, LANES), 0)
    live = jnp.concatenate(
        [slots < counts_ref[source, frame] for source in range(sources)], axis=0)
    lower = lax.broadcasted_iota(jnp.int32, (tokens, LANES), 1) < IDM_DIM
    scale = IDM_DIM ** (-0.5) * LOG2E
    for c in range(0, columns, LANES):
        k = jnp.concatenate([ref[0, :, c:c + LANES] for ref in refs[:sources]], axis=0)
        q = refs[0][0, :, c:c + LANES]
        zero = jnp.zeros_like(q)
        q = jnp.concatenate([jnp.where(lower, q, zero), jnp.where(lower, zero, q)], axis=0)
        v = jnp.concatenate(
            [jnp.where(live, k, jnp.zeros_like(k)), live.astype(k.dtype)], axis=1)
        scores = lax.dot_general(q, k, (((1,), (1,)), ((), ())), preferred_element_type=jnp.float32)
        weights = jnp.exp2(scores * scale).astype(jnp.bfloat16)
        mixed = jnp.dot(weights, v, preferred_element_type=jnp.float32)
        result = mixed[:, :LANES] / mixed[:, LANES:]
        out_ref[0, :, c:c + LANES] = jnp.where(
            lower, result[:tokens], result[tokens:]).astype(out_ref.dtype)


def partner_attention(counts, blocks):
    frames, tokens, columns = blocks[0].shape
    spec = pl.BlockSpec((1, tokens, columns), lambda f: (f, 0, 0))
    return pl.pallas_call(
        functools.partial(partner_kernel, len(blocks)),
        out_shape=jax.ShapeDtypeStruct(blocks[0].shape, jnp.bfloat16),
        grid=(frames,),
        in_specs=[pl.BlockSpec(memory_space=pltpu.SMEM)] + [spec] * len(blocks),
        out_specs=spec,
        compiler_params=pltpu.CompilerParams(vmem_limit_bytes=32 * 2 ** 20),
    )(counts, *blocks)


def local(mesh, queries, keyvals, proj_weight, norm_gain, frame_counts):
    normed = normed_latent(mesh, queries, keyvals, proj_weight, norm_gain, frame_counts)
    distance = PARTNER // queries.shape[0]
    blocks, counts = [normed], [frame_counts]
    for steps in (distance, -distance):
        if distance < mesh.shape["tm"]:
            block, count = passed_along((normed, frame_counts), "tm", steps)
            blocks.append(block)
            counts.append(count)
    return partner_attention(jnp.stack(counts), blocks)


def solution(mesh):
    in_specs = (
        P(("clip", "tm"), "tile", None),
        P(None, ("clip", "tm"), "tile", None),
        P("tm", "tile"),
        P("tile"),
        P(("clip", "tm")),
    )
    out_specs = P(("clip", "tm"), None, "tile")
    return jax.shard_map(
        functools.partial(local, mesh), mesh=mesh, in_specs=in_specs, out_specs=out_specs,
        check_vma=False)
```

```python
import functools
import math

import jax
import jax.numpy as jnp
from jax import lax
from jax.experimental import pallas as pl
from jax.experimental.pallas import tpu as pltpu
from jax.sharding import PartitionSpec as P

QHEADS = 16
KVHEADS = 4
HEAD_DIM = 128
IDM_DIM = 64
WINDOW = 4
PARTNER = 16
LEAD = WINDOW - 1
LANES = 128
TILE_ROWS = 16
DEAD = -1e30
LOG2E = math.log2(math.e)
MESH = pl.DeviceIdType.MESH


def passed_along(value, axis, steps):
    count = lax.axis_size(axis)
    initial, last = (max(0, -steps), min(count, count - steps))
    return lax.ppermute(value, axis, [(source, source + steps) for source in range(initial, last)])


def columns_of(mesh):
    place = mesh.axis_names.index("tm")
    line = mesh.devices.transpose(
        [place] + [i for i in range(mesh.devices.ndim) if i != place]
    ).reshape(mesh.shape["tm"], -1)[:, 0]
    coords = [getattr(device, "coords", None) for device in line]
    if coords[0] is None or len(line) == 1:
        return 1
    moved = [i for i in range(len(coords[0])) if coords[0][i] != coords[1][i]]
    if len(moved) != 1:
        return 1
    columns = len({c[moved[0]] for c in coords})
    return columns if len(line) % columns == 0 else 1


def halo_plan(frames):
    plan, covered, hop = [], 0, 1
    while covered < LEAD:
        needed = min(frames, LEAD - covered)
        covered += needed
        plan.append((hop, needed, LEAD - covered))
        hop += 1
    return plan


def relayed(plan, x_count, n):
    return x_count == 2 and n % 2 == 0 and len(plan) == 2 and plan[0][1] > plan[1][1]


def ring_chunks(rows, clip, clips):
    over = clips == 2 and rows % (2 * TILE_ROWS) == 0
    start, size = (clip * (rows // 2), rows // 2) if over else (0, rows)
    if size % (2 * TILE_ROWS):
        return [(start, size, over)]
    return [(start, size // 2, over), (start + size // 2, size // 2, over)]


def latent_kernel(
    n, clips, tiles, x_count,
    counts_ref, q_ref, kv_ref, w_ref, gain_ref, out_ref,
    q_buf, kv_win, stash, w_full, att, total_ref, counts, bias,
    local_sem, halo_send, halo_recv, count_send, count_recv,
    ring_send, ring_recv, clip_send, clip_recv, tile_send, tile_recv,
):
    clip, tm, tile = lax.axis_index("clip"), lax.axis_index("tm"), lax.axis_index("tile")
    frames, tokens, width = q_ref.shape
    rows = w_ref.shape[0]
    groups = QHEADS // KVHEADS
    plan = halo_plan(frames)
    z_count = n // x_count

    def place_of(index):
        x, z = lax.rem(index, x_count), index // x_count
        return x * z_count + z + lax.rem(x, 2) * (z_count - 1 - 2 * z)

    def index_of(place):
        place = lax.rem(place + 2 * n, n)
        x, z = place // z_count, lax.rem(place, z_count)
        return (z + lax.rem(x, 2) * (z_count - 1 - 2 * z)) * x_count + x

    place = place_of(tm)
    ends = (index_of(place + 1), index_of(place - 1))

    own_copies = [
        pltpu.make_async_copy(kv_ref, kv_win.at[:, LEAD:LEAD + frames], local_sem.at[0]),
        pltpu.make_async_copy(q_ref, q_buf, local_sem.at[1]),
        pltpu.make_async_copy(w_ref, w_full.at[tm], local_sem.at[2]),
    ]
    for copy in own_copies:
        copy.start()

    barrier = pltpu.get_barrier_semaphore()
    expected = 0
    if n > 1:
        for end in ends:
            pl.semaphore_signal(barrier, inc=1, device_id={"tm": end}, device_id_type=MESH)
            expected += 1
    if clips == 2:
        pl.semaphore_signal(barrier, inc=1, device_id={"clip": 1 - clip}, device_id_type=MESH)
        expected += 1
    if tiles == 2:
        pl.semaphore_signal(barrier, inc=1, device_id={"tile": 1 - tile}, device_id_type=MESH)
        expected += 1
    for hop, _, _ in plan:
        @pl.when(tm + hop < n)
        def _():
            pl.semaphore_signal(barrier, inc=1, device_id={"tm": tm + hop}, device_id_type=MESH)

        @pl.when(tm >= hop)
        def _():
            pl.semaphore_signal(barrier, inc=1, device_id={"tm": tm - hop}, device_id_type=MESH)

        expected = expected + jnp.where(tm + hop < n, 1, 0) + jnp.where(tm >= hop, 1, 0)
    for f in range(frames):
        counts[0, f:f + 1, :] = jnp.full((1, LANES), counts_ref[f], jnp.int32)
    pl.semaphore_wait(barrier, expected)

    count_copies = []
    for i, (hop, _, _) in enumerate(plan):
        count_copies.append((hop, pltpu.make_async_remote_copy(
            src_ref=counts.at[0], dst_ref=counts.at[hop],
            send_sem=count_send.at[i], recv_sem=count_recv.at[i],
            device_id={"tm": lax.rem(tm + hop, n)}, device_id_type=MESH)))
    for hop, copy in count_copies:
        pl.when(tm + hop < n)(copy.start)

    def halo_copy(role, arrival, g, source, first, count, place_at, hop):
        span = pl.ds(g * HEAD_DIM, HEAD_DIM)
        target = stash if place_at is None else kv_win.at[:, place_at:place_at + count]
        return pltpu.make_async_remote_copy(
            src_ref=source.at[:, first:first + count, :, span],
            dst_ref=target.at[:, :, :, span],
            send_sem=halo_send.at[role * KVHEADS + g],
            recv_sem=halo_recv.at[arrival * KVHEADS + g],
            device_id={"tm": lax.rem(tm + hop + n, n)}, device_id_type=MESH)

    firsts, relays, arrivals = [[] for _ in range(KVHEADS)], [], []
    if relayed(plan, x_count, n):
        (_, needed, start), (_, last, start2) = plan
        rest = needed - last
        even, odd = lax.rem(tm, 2) == 0, lax.rem(tm, 2) == 1
        up, down = tm + 2 < n, tm >= 2
        for g in range(KVHEADS):
            firsts[g] += [
                (halo_copy(2, 2, g, kv_ref, frames - last, last, start2, 2), up),
                (halo_copy(3, 3, g, kv_ref, frames - needed, rest, None, -1),
                 jnp.logical_and(odd, up)),
                (halo_copy(0, 0, g, kv_ref, frames - needed, rest, start, 1), even),
                (halo_copy(1, 1, g, kv_ref, frames - last, last, start + rest, 1), even),
            ]
            relays.append([
                (halo_copy(4, 0, g, stash, 0, rest, start, 2), jnp.logical_and(even, up), 3),
                (halo_copy(5, 1, g, kv_win, start2, last, start + rest, -1),
                 jnp.logical_and(odd, down), 2),
            ])
            arrivals.append([
                (0, tm >= 1, rest, start), (1, tm >= 1, last, start + rest),
                (2, jnp.logical_and(even, down), last, start2),
            ])
    else:
        for g in range(KVHEADS):
            for i, (hop, needed, start) in enumerate(plan):
                firsts[g].append((
                    halo_copy(i, i, g, kv_ref, frames - needed, needed, start, hop), tm + hop < n))
            relays.append([])
            arrivals.append([
                (i, tm >= hop, needed, start) for i, (hop, needed, start) in enumerate(plan)])

    def issue(g):
        if g < KVHEADS:
            for copy, mine in firsts[g]:
                pl.when(mine)(copy.start)

    def arrival_of(arrival, g, count, place_at):
        return halo_copy(0, arrival, g, kv_ref, 0, count, place_at, 1)

    def relay(g):
        for copy, mine, arrival in relays[g]:
            @pl.when(mine)
            def _():
                count, place_at = (rest, None) if arrival == 3 else (last, start2)
                arrival_of(arrival, g, count, place_at).wait_recv()
                copy.start()

    def arrive(g):
        for arrival, mine, count, place_at in arrivals[g]:
            pl.when(mine)(arrival_of(arrival, g, count, place_at).wait_recv)

    chunks = ring_chunks(rows, clip, clips)
    steps = n // 2
    started, later = [], []

    def ring_copy(way, step, c):
        start, size, _ = chunks[c]
        owner = index_of(place - step * (1 - 2 * way))
        span = pl.ds(start if isinstance(start, int) else pl.multiple_of(start, TILE_ROWS), size)
        slot = (way * max(steps, 1) + step) * len(chunks) + c
        return pltpu.make_async_remote_copy(
            src_ref=w_ref.at[span] if step == 0 else w_full.at[owner, span],
            dst_ref=w_full.at[owner, span],
            send_sem=ring_send.at[slot], recv_sem=ring_recv.at[slot],
            device_id={"tm": ends[way]}, device_id_type=MESH)

    def goes(way, step, c):
        return n % 2 == 1 or step < steps - 1 or c % 2 == way

    def send_step(way, step, c):
        if step < steps and goes(way, step, c):
            copy = ring_copy(way, step, c)
            copy.start()
            started.append(copy)

    def take_step(step):
        for c in range(len(chunks)):
            for way in range(2):
                if not goes(way, step, c):
                    continue
                ring_copy(way, step, c).wait_recv()
                send_step(way, step + 1, c)
                start, size, over = chunks[c]
                if over:
                    owner = index_of(place - (step + 1) * (1 - 2 * way))
                    span = pl.ds(pl.multiple_of(start, TILE_ROWS), size)
                    slot = (way * steps + step) * len(chunks) + c
                    copy = pltpu.make_async_remote_copy(
                        src_ref=w_full.at[owner, span], dst_ref=w_full.at[owner, span],
                        send_sem=clip_send.at[slot], recv_sem=clip_recv.at[slot],
                        device_id={"clip": 1 - clip}, device_id_type=MESH)
                    copy.start()
                    later.append(copy)

    issue(0)
    for c in range(len(chunks)):
        for way in range(2):
            send_step(way, 0, c)
    issue(1)

    for hop, needed, start in plan:
        @pl.when(tm < hop)
        def _():
            counts[hop] = jnp.zeros(counts.shape[1:], jnp.int32)
            kv_win[:, start:start + needed] = jnp.zeros(
                (2, needed) + kv_win.shape[2:], kv_win.dtype)

    for hop, copy in count_copies:
        pl.when(tm >= hop)(copy.wait_recv)
    own_copies[0].wait()
    own_copies[1].wait()

    slots = tile * tokens + lax.broadcasted_iota(jnp.int32, (tokens, LANES), 0)
    first_lane = lax.broadcasted_iota(jnp.int32, (tokens, LANES), 1) == 0
    for w in range(LEAD + frames):
        if w >= LEAD:
            row = counts[0, w - LEAD:w - LEAD + 1, :]
        else:
            hop, needed, start = [p for p in plan if p[2] <= w < p[2] + p[1]][0]
            at = frames - needed + w - start
            row = counts[hop, at:at + 1, :]
        bias[w] = jnp.where(
            jnp.logical_and(first_lane, slots >= row), DEAD, 0.0).astype(bias.dtype)

    keys = WINDOW * tokens
    unit_lane = (
        lax.broadcasted_iota(jnp.int32, (groups * tokens, LANES), 1) == 0
    ).astype(jnp.bfloat16)
    ones = jnp.ones((keys, LANES), jnp.bfloat16)
    scale = HEAD_DIM ** (-0.5) * LOG2E
    exchanged = []
    taken = 0
    for unit in range(KVHEADS * frames):
        g, f = unit // frames, unit % frames
        if f == 0:
            relay(g)
            if taken < steps - 1:
                take_step(taken)
                taken += 1
            issue(g + 2)
            arrive(g)
        span = slice(g * HEAD_DIM, (g + 1) * HEAD_DIM)
        k = kv_win[0, f:f + WINDOW, :, span].reshape(keys, HEAD_DIM)
        v = kv_win[1, f:f + WINDOW, :, span].reshape(keys, HEAD_DIM)
        k = jnp.concatenate([k, bias[f:f + WINDOW].reshape(keys, LANES)], axis=1)
        v = jnp.concatenate([v, ones], axis=1)
        q = jnp.concatenate(
            [q_buf[f, :, (g * groups + i) * HEAD_DIM:(g * groups + i + 1) * HEAD_DIM]
             for i in range(groups)], axis=0)
        q = jnp.concatenate([q, unit_lane], axis=1)
        scores = lax.dot_general(q, k, (((1,), (1,)), ((), ())), preferred_element_type=jnp.float32)
        top = jnp.max(scores, axis=-1, keepdims=True)
        weights = jnp.exp2((scores - top) * scale).astype(jnp.bfloat16)
        mixed = jnp.dot(weights, v, preferred_element_type=jnp.float32)
        result = (mixed[:, :HEAD_DIM] / mixed[:, HEAD_DIM:]).astype(jnp.bfloat16)
        for i in range(groups):
            at = (g * groups + i) * HEAD_DIM
            att[f, tile, :, at:at + HEAD_DIM] = result[i * tokens:(i + 1) * tokens]
        if tiles == 2:
            part = att.at[f, tile, :, g * groups * HEAD_DIM:(g + 1) * groups * HEAD_DIM]
            copy = pltpu.make_async_remote_copy(
                src_ref=part, dst_ref=part,
                send_sem=tile_send.at[unit], recv_sem=tile_recv.at[unit],
                device_id={"tile": 1 - tile}, device_id_type=MESH)
            copy.start()
            exchanged.append(copy)
    while taken < steps - 1:
        take_step(taken)
        taken += 1

    columns = w_ref.shape[1]
    same = (
        lax.rem(lax.broadcasted_iota(jnp.int32, (2 * LANES, LANES), 0), LANES) // IDM_DIM
        == lax.broadcasted_iota(jnp.int32, (2 * LANES, LANES), 1) // IDM_DIM
    ).astype(jnp.bfloat16)
    own_copies[2].wait()
    for copy in exchanged:
        copy.wait_recv()

    def projected(f, owners):
        if owners is None:
            return jnp.dot(
                att[f].reshape(tiles * tokens, width), w_full[...].reshape(n * rows, columns),
                preferred_element_type=jnp.float32)
        parts = []
        for owner in owners:
            span = pl.ds(pl.multiple_of(owner * rows, LANES), rows)
            parts.append(jnp.dot(
                att[f, :, :, span].reshape(tiles * tokens, rows), w_full[owner],
                preferred_element_type=jnp.float32))
        return sum(parts)

    first_wave, last_wave = [tm], None
    by_clip = list(later)
    if rows % LANES == 0 and steps > 1:
        for step in range(steps - 1):
            first_wave += [index_of(place - step - 1), index_of(place + step + 1)]
        last_wave = [index_of(place - steps)]
        if n % 2:
            last_wave.append(index_of(place + steps))
        for copy in by_clip:
            copy.wait_recv()
        for f in range(frames):
            total_ref[f] = projected(f, first_wave)
    else:
        by_clip = []
    if steps:
        take_step(steps - 1)
    for copy in later[len(by_clip):]:
        copy.wait_recv()
    for f in range(frames):
        latent = projected(f, last_wave)
        if last_wave is not None:
            latent = latent + total_ref[f]
        latent = latent.astype(jnp.bfloat16).astype(jnp.float32)
        for c in range(0, columns, LANES):
            value = latent[:, c:c + LANES]
            square = value * value
            high = square.astype(jnp.bfloat16)
            low = (square - high.astype(jnp.float32)).astype(jnp.bfloat16)
            total = jnp.dot(
                jnp.concatenate([high, low], axis=1), same, preferred_element_type=jnp.float32)
            scaled = value * lax.rsqrt(total * (1.0 / IDM_DIM) + 1e-6) * gain_ref[:, c:c + LANES]
            out_ref[f, :, c:c + LANES] = scaled.astype(out_ref.dtype)

    for copy in started + later + exchanged:
        copy.wait_send()
    for hop, copy in count_copies:
        pl.when(tm + hop < n)(copy.wait_send)
    for group in firsts + relays:
        for entry in group:
            pl.when(entry[1])(entry[0].wait_send)


def normed_latent(mesh, queries, keyvals, proj_weight, norm_gain, frame_counts):
    n, clips, tiles = (mesh.shape[a] for a in ("tm", "clip", "tile"))
    frames, tokens, width = queries.shape
    rows, columns = proj_weight.shape
    plan = halo_plan(frames)
    hops = len(plan)
    rest = max(1, plan[0][1] - plan[1][1]) if hops > 1 else 1
    roles = max(6, hops) * KVHEADS
    steps = max(1, n // 2)
    units = frames * KVHEADS
    dma = pltpu.SemaphoreType.DMA
    hbm = pl.BlockSpec(memory_space=pltpu.HBM)
    vmem = pl.BlockSpec(memory_space=pltpu.VMEM)
    bf16 = jnp.bfloat16
    flops = frames * tokens * width * 4 * WINDOW * tokens + 2 * frames * tiles * tokens * width * columns
    return pl.pallas_call(
        functools.partial(latent_kernel, n, clips, tiles, columns_of(mesh)),
        out_shape=jax.ShapeDtypeStruct((frames, tiles * tokens, columns), bf16),
        in_specs=[pl.BlockSpec(memory_space=pltpu.SMEM), hbm, hbm, hbm, vmem],
        out_specs=vmem,
        scratch_shapes=[
            pltpu.VMEM(queries.shape, bf16),
            pltpu.VMEM((2, LEAD + frames) + keyvals.shape[2:], bf16),
            pltpu.VMEM((2, rest) + keyvals.shape[2:], bf16),
            pltpu.VMEM((n, rows, columns), bf16),
            pltpu.VMEM((frames, tiles, tokens, width), bf16),
            pltpu.VMEM((frames, tiles * tokens, columns), jnp.float32),
            pltpu.VMEM((hops + 1, max(8, frames), LANES), jnp.int32),
            pltpu.VMEM((LEAD + frames, tokens, LANES), bf16),
            dma((3,)), dma((roles,)), dma((roles,)), dma((hops,)), dma((hops,)),
            dma((4 * steps,)), dma((4 * steps,)), dma((4 * steps,)), dma((4 * steps,)),
            dma((units,)), dma((units,)),
        ],
        compiler_params=pltpu.CompilerParams(
            collective_id=0, has_side_effects=True, vmem_limit_bytes=60 * 2 ** 20),
        cost_estimate=pl.CostEstimate(
            flops=flops, bytes_accessed=8 * 2 ** 20, transcendentals=0),
    )(frame_counts, queries, keyvals, proj_weight, norm_gain.reshape(1, -1))


def partner_kernel(sources, counts_ref, *refs):
    out_ref = refs[-1]
    frame = pl.program_id(0)
    tokens, columns = out_ref.shape[1:]
    keys = sources * tokens
    slots = lax.broadcasted_iota(jnp.int32, (tokens, LANES), 0)
    live = jnp.concatenate(
        [slots < counts_ref[source, frame] for source in range(sources)], axis=0)
    lower = lax.broadcasted_iota(jnp.int32, (tokens, LANES), 1) < IDM_DIM
    scale = IDM_DIM ** (-0.5) * LOG2E
    for c in range(0, columns, LANES):
        k = jnp.concatenate([ref[0, :, c:c + LANES] for ref in refs[:sources]], axis=0)
        q = refs[0][0, :, c:c + LANES]
        zero = jnp.zeros_like(q)
        q = jnp.concatenate([jnp.where(lower, q, zero), jnp.where(lower, zero, q)], axis=0)
        v = jnp.concatenate(
            [jnp.where(live, k, jnp.zeros_like(k)), live.astype(k.dtype)], axis=1)
        scores = lax.dot_general(q, k, (((1,), (1,)), ((), ())), preferred_element_type=jnp.float32)
        weights = jnp.exp2(scores * scale).astype(jnp.bfloat16)
        mixed = jnp.dot(weights, v, preferred_element_type=jnp.float32)
        result = mixed[:, :LANES] / mixed[:, LANES:]
        out_ref[0, :, c:c + LANES] = jnp.where(
            lower, result[:tokens], result[tokens:]).astype(out_ref.dtype)


def partner_attention(counts, blocks):
    frames, tokens, columns = blocks[0].shape
    spec = pl.BlockSpec((1, tokens, columns), lambda f: (f, 0, 0))
    return pl.pallas_call(
        functools.partial(partner_kernel, len(blocks)),
        out_shape=jax.ShapeDtypeStruct(blocks[0].shape, jnp.bfloat16),
        grid=(frames,),
        in_specs=[pl.BlockSpec(memory_space=pltpu.SMEM)] + [spec] * len(blocks),
        out_specs=spec,
        compiler_params=pltpu.CompilerParams(vmem_limit_bytes=60 * 2 ** 20),
    )(counts, *blocks)


def local(mesh, queries, keyvals, proj_weight, norm_gain, frame_counts):
    normed = normed_latent(mesh, queries, keyvals, proj_weight, norm_gain, frame_counts)
    distance = PARTNER // queries.shape[0]
    blocks, counts = [normed], [frame_counts]
    for steps in (distance, -distance):
        if distance < mesh.shape["tm"]:
            block, count = passed_along((normed, frame_counts), "tm", steps)
            blocks.append(block)
            counts.append(count)
    return partner_attention(jnp.stack(counts), blocks)


def solution(mesh):
    in_specs = (
        P(("clip", "tm"), "tile", None),
        P(None, ("clip", "tm"), "tile", None),
        P("tm", "tile"),
        P("tile"),
        P(("clip", "tm")),
    )
    out_specs = P(("clip", "tm"), None, "tile")
    return jax.shard_map(
        functools.partial(local, mesh), mesh=mesh, in_specs=in_specs, out_specs=out_specs,
        check_vma=False)
```

```python
import functools
import math

import jax
import jax.numpy as jnp
from jax import lax
from jax.experimental import pallas as pl
from jax.experimental.pallas import tpu as pltpu
from jax.sharding import PartitionSpec as P

QHEADS = 16
KVHEADS = 4
HEAD_DIM = 128
IDM_DIM = 64
WINDOW = 4
PARTNER = 16
LEAD = WINDOW - 1
LANES = 128
TILE_ROWS = 16
DEAD = -1e30
LOG2E = math.log2(math.e)
MESH = pl.DeviceIdType.MESH


def passed_along(value, axis, steps):
    count = lax.axis_size(axis)
    initial, last = (max(0, -steps), min(count, count - steps))
    return lax.ppermute(value, axis, [(source, source + steps) for source in range(initial, last)])


def columns_of(mesh):
    place = mesh.axis_names.index("tm")
    line = mesh.devices.transpose(
        [place] + [i for i in range(mesh.devices.ndim) if i != place]
    ).reshape(mesh.shape["tm"], -1)[:, 0]
    coords = [getattr(device, "coords", None) for device in line]
    if coords[0] is None or len(line) == 1:
        return 1
    moved = [i for i in range(len(coords[0])) if coords[0][i] != coords[1][i]]
    if len(moved) != 1:
        return 1
    columns = len({c[moved[0]] for c in coords})
    return columns if len(line) % columns == 0 else 1


def halo_plan(frames):
    plan, covered, hop = [], 0, 1
    while covered < LEAD:
        needed = min(frames, LEAD - covered)
        covered += needed
        plan.append((hop, needed, LEAD - covered))
        hop += 1
    return plan


def relayed(plan, x_count, n):
    return x_count == 2 and n % 2 == 0 and len(plan) == 2 and plan[0][1] > plan[1][1]


def ring_chunks(rows, clip, clips):
    over = clips == 2 and rows % (2 * TILE_ROWS) == 0
    start, size = (clip * (rows // 2), rows // 2) if over else (0, rows)
    if size % (2 * TILE_ROWS):
        return [(start, size, over)]
    return [(start, size // 2, over), (start + size // 2, size // 2, over)]


def latent_kernel(
    n, clips, tiles, x_count,
    counts_ref, q_ref, kv_ref, w_ref, gain_ref, out_ref,
    q_buf, kv_win, stash, w_full, att, total_ref, counts, bias,
    local_sem, halo_send, halo_recv, count_send, count_recv,
    ring_send, ring_recv, clip_send, clip_recv, tile_send, tile_recv,
):
    clip, tm, tile = lax.axis_index("clip"), lax.axis_index("tm"), lax.axis_index("tile")
    frames, tokens, width = q_ref.shape
    rows = w_ref.shape[0]
    groups = QHEADS // KVHEADS
    plan = halo_plan(frames)
    z_count = n // x_count

    def place_of(index):
        x, z = lax.rem(index, x_count), index // x_count
        return x * z_count + z + lax.rem(x, 2) * (z_count - 1 - 2 * z)

    def index_of(place):
        place = lax.rem(place + 2 * n, n)
        x, z = place // z_count, lax.rem(place, z_count)
        return (z + lax.rem(x, 2) * (z_count - 1 - 2 * z)) * x_count + x

    place = place_of(tm)
    ends = (index_of(place + 1), index_of(place - 1))

    own_copies = [
        pltpu.make_async_copy(kv_ref, kv_win.at[:, LEAD:LEAD + frames], local_sem.at[0]),
        pltpu.make_async_copy(q_ref, q_buf, local_sem.at[1]),
        pltpu.make_async_copy(w_ref, w_full.at[tm], local_sem.at[2]),
    ]
    for copy in own_copies:
        copy.start()

    barrier = pltpu.get_barrier_semaphore()
    expected = 0
    if n > 1:
        for end in ends:
            pl.semaphore_signal(barrier, inc=1, device_id={"tm": end}, device_id_type=MESH)
            expected += 1
    if clips == 2:
        pl.semaphore_signal(barrier, inc=1, device_id={"clip": 1 - clip}, device_id_type=MESH)
        expected += 1
    if tiles == 2:
        pl.semaphore_signal(barrier, inc=1, device_id={"tile": 1 - tile}, device_id_type=MESH)
        expected += 1
    for hop, _, _ in plan:
        @pl.when(tm + hop < n)
        def _():
            pl.semaphore_signal(barrier, inc=1, device_id={"tm": tm + hop}, device_id_type=MESH)

        @pl.when(tm >= hop)
        def _():
            pl.semaphore_signal(barrier, inc=1, device_id={"tm": tm - hop}, device_id_type=MESH)

        expected = expected + jnp.where(tm + hop < n, 1, 0) + jnp.where(tm >= hop, 1, 0)
    for f in range(frames):
        counts[0, f:f + 1, :] = jnp.full((1, LANES), counts_ref[f], jnp.int32)
    pl.semaphore_wait(barrier, expected)

    count_copies = []
    for i, (hop, _, _) in enumerate(plan):
        count_copies.append((hop, pltpu.make_async_remote_copy(
            src_ref=counts.at[0], dst_ref=counts.at[hop],
            send_sem=count_send.at[i], recv_sem=count_recv.at[i],
            device_id={"tm": lax.rem(tm + hop, n)}, device_id_type=MESH)))
    for hop, copy in count_copies:
        pl.when(tm + hop < n)(copy.start)

    def halo_copy(role, arrival, g, source, first, count, place_at, hop):
        span = pl.ds(g * HEAD_DIM, HEAD_DIM)
        target = stash if place_at is None else kv_win.at[:, place_at:place_at + count]
        return pltpu.make_async_remote_copy(
            src_ref=source.at[:, first:first + count, :, span],
            dst_ref=target.at[:, :, :, span],
            send_sem=halo_send.at[role * KVHEADS + g],
            recv_sem=halo_recv.at[arrival * KVHEADS + g],
            device_id={"tm": lax.rem(tm + hop + n, n)}, device_id_type=MESH)

    firsts, relays, arrivals = [[] for _ in range(KVHEADS)], [], []
    if relayed(plan, x_count, n):
        (_, needed, start), (_, last, start2) = plan
        rest = needed - last
        even, odd = lax.rem(tm, 2) == 0, lax.rem(tm, 2) == 1
        up, down = tm + 2 < n, tm >= 2
        for g in range(KVHEADS):
            firsts[g] += [
                (halo_copy(2, 2, g, kv_ref, frames - last, last, start2, 2), up),
                (halo_copy(3, 3, g, kv_ref, frames - needed, rest, None, -1),
                 jnp.logical_and(odd, up)),
                (halo_copy(0, 0, g, kv_ref, frames - needed, rest, start, 1), even),
                (halo_copy(1, 1, g, kv_ref, frames - last, last, start + rest, 1), even),
            ]
            relays.append([
                (halo_copy(4, 0, g, stash, 0, rest, start, 2), jnp.logical_and(even, up), 3),
                (halo_copy(5, 1, g, kv_win, start2, last, start + rest, -1),
                 jnp.logical_and(odd, down), 2),
            ])
            arrivals.append([
                (0, tm >= 1, rest, start), (1, tm >= 1, last, start + rest),
                (2, jnp.logical_and(even, down), last, start2),
            ])
    else:
        for g in range(KVHEADS):
            for i, (hop, needed, start) in enumerate(plan):
                firsts[g].append((
                    halo_copy(i, i, g, kv_ref, frames - needed, needed, start, hop), tm + hop < n))
            relays.append([])
            arrivals.append([
                (i, tm >= hop, needed, start) for i, (hop, needed, start) in enumerate(plan)])

    def issue(g):
        if g < KVHEADS:
            for copy, mine in firsts[g]:
                pl.when(mine)(copy.start)

    def arrival_of(arrival, g, count, place_at):
        return halo_copy(0, arrival, g, kv_ref, 0, count, place_at, 1)

    def relay(g):
        for copy, mine, arrival in relays[g]:
            @pl.when(mine)
            def _():
                count, place_at = (rest, None) if arrival == 3 else (last, start2)
                arrival_of(arrival, g, count, place_at).wait_recv()
                copy.start()

    def arrive(g):
        for arrival, mine, count, place_at in arrivals[g]:
            pl.when(mine)(arrival_of(arrival, g, count, place_at).wait_recv)

    chunks = ring_chunks(rows, clip, clips)
    steps = n // 2
    started, later = [], []

    def ring_copy(way, step, c):
        start, size, _ = chunks[c]
        owner = index_of(place - step * (1 - 2 * way))
        span = pl.ds(start if isinstance(start, int) else pl.multiple_of(start, TILE_ROWS), size)
        slot = (way * max(steps, 1) + step) * len(chunks) + c
        return pltpu.make_async_remote_copy(
            src_ref=w_ref.at[span] if step == 0 else w_full.at[owner, span],
            dst_ref=w_full.at[owner, span],
            send_sem=ring_send.at[slot], recv_sem=ring_recv.at[slot],
            device_id={"tm": ends[way]}, device_id_type=MESH)

    def goes(way, step, c):
        return n % 2 == 1 or step < steps - 1 or c % 2 == way

    def send_step(way, step, c):
        if step < steps and goes(way, step, c):
            copy = ring_copy(way, step, c)
            copy.start()
            started.append(copy)

    def take(step, c):
        if c < len(chunks):
            for way in range(2):
                if not goes(way, step, c):
                    continue
                ring_copy(way, step, c).wait_recv()
                send_step(way, step + 1, c)
                start, size, over = chunks[c]
                if over:
                    owner = index_of(place - (step + 1) * (1 - 2 * way))
                    span = pl.ds(pl.multiple_of(start, TILE_ROWS), size)
                    slot = (way * steps + step) * len(chunks) + c
                    copy = pltpu.make_async_remote_copy(
                        src_ref=w_full.at[owner, span], dst_ref=w_full.at[owner, span],
                        send_sem=clip_send.at[slot], recv_sem=clip_recv.at[slot],
                        device_id={"clip": 1 - clip}, device_id_type=MESH)
                    copy.start()
                    later.append(copy)

    for c in range(len(chunks)):
        for way in range(2):
            send_step(way, 0, c)
        if c == 0:
            issue(0)
    issue(1)

    for hop, needed, start in plan:
        @pl.when(tm < hop)
        def _():
            counts[hop] = jnp.zeros(counts.shape[1:], jnp.int32)
            kv_win[:, start:start + needed] = jnp.zeros(
                (2, needed) + kv_win.shape[2:], kv_win.dtype)

    for hop, copy in count_copies:
        pl.when(tm >= hop)(copy.wait_recv)
    own_copies[0].wait()
    own_copies[1].wait()

    slots = tile * tokens + lax.broadcasted_iota(jnp.int32, (tokens, LANES), 0)
    first_lane = lax.broadcasted_iota(jnp.int32, (tokens, LANES), 1) == 0
    for w in range(LEAD + frames):
        if w >= LEAD:
            row = counts[0, w - LEAD:w - LEAD + 1, :]
        else:
            hop, needed, start = [p for p in plan if p[2] <= w < p[2] + p[1]][0]
            at = frames - needed + w - start
            row = counts[hop, at:at + 1, :]
        bias[w] = jnp.where(
            jnp.logical_and(first_lane, slots >= row), DEAD, 0.0).astype(bias.dtype)

    keys = WINDOW * tokens
    unit_lane = (
        lax.broadcasted_iota(jnp.int32, (groups * tokens, LANES), 1) == 0
    ).astype(jnp.bfloat16)
    ones = jnp.ones((keys, LANES), jnp.bfloat16)
    scale = HEAD_DIM ** (-0.5) * LOG2E
    exchanged = []
    taken = 0
    relay(0)
    for unit in range(KVHEADS * frames):
        g, f = unit // frames, unit % frames
        if f == 0:
            if taken < steps - 1:
                take(taken, 0)
            issue(g + 2)
            arrive(g)
        if f == frames - 1:
            if taken < steps - 1:
                take(taken, 1)
                taken += 1
            if g + 1 < KVHEADS:
                relay(g + 1)
        span = slice(g * HEAD_DIM, (g + 1) * HEAD_DIM)
        k = kv_win[0, f:f + WINDOW, :, span].reshape(keys, HEAD_DIM)
        v = kv_win[1, f:f + WINDOW, :, span].reshape(keys, HEAD_DIM)
        k = jnp.concatenate([k, bias[f:f + WINDOW].reshape(keys, LANES)], axis=1)
        v = jnp.concatenate([v, ones], axis=1)
        q = jnp.concatenate(
            [q_buf[f, :, (g * groups + i) * HEAD_DIM:(g * groups + i + 1) * HEAD_DIM]
             for i in range(groups)], axis=0)
        q = jnp.concatenate([q, unit_lane], axis=1)
        scores = lax.dot_general(q, k, (((1,), (1,)), ((), ())), preferred_element_type=jnp.float32)
        top = jnp.max(scores, axis=-1, keepdims=True)
        weights = jnp.exp2((scores - top) * scale).astype(jnp.bfloat16)
        mixed = jnp.dot(weights, v, preferred_element_type=jnp.float32)
        result = (mixed[:, :HEAD_DIM] / mixed[:, HEAD_DIM:]).astype(jnp.bfloat16)
        for i in range(groups):
            at = (g * groups + i) * HEAD_DIM
            att[f, tile, :, at:at + HEAD_DIM] = result[i * tokens:(i + 1) * tokens]
        if tiles == 2:
            part = att.at[f, tile, :, g * groups * HEAD_DIM:(g + 1) * groups * HEAD_DIM]
            copy = pltpu.make_async_remote_copy(
                src_ref=part, dst_ref=part,
                send_sem=tile_send.at[unit], recv_sem=tile_recv.at[unit],
                device_id={"tile": 1 - tile}, device_id_type=MESH)
            copy.start()
            exchanged.append(copy)
    while taken < steps:
        before_last = list(later)
        take(taken, 0)
        take(taken, 1)
        taken += 1

    columns = w_ref.shape[1]
    same = (
        lax.rem(lax.broadcasted_iota(jnp.int32, (2 * LANES, LANES), 0), LANES) // IDM_DIM
        == lax.broadcasted_iota(jnp.int32, (2 * LANES, LANES), 1) // IDM_DIM
    ).astype(jnp.bfloat16)
    own_copies[2].wait()
    for copy in exchanged:
        copy.wait_recv()

    def projected(f, owners):
        if owners is None:
            return jnp.dot(
                att[f].reshape(tiles * tokens, width), w_full[...].reshape(n * rows, columns),
                preferred_element_type=jnp.float32)
        parts = []
        for owner in owners:
            span = pl.ds(pl.multiple_of(owner * rows, LANES), rows)
            parts.append(jnp.dot(
                att[f, :, :, span].reshape(tiles * tokens, rows), w_full[owner],
                preferred_element_type=jnp.float32))
        return sum(parts)

    first_wave, last_wave = [tm], None
    by_clip = before_last if steps else []
    if rows % LANES == 0 and steps > 1:
        for step in range(steps - 1):
            first_wave += [index_of(place - step - 1), index_of(place + step + 1)]
        last_wave = [index_of(place - steps)]
        if n % 2:
            last_wave.append(index_of(place + steps))
        for copy in by_clip:
            copy.wait_recv()
        for f in range(frames):
            total_ref[f] = projected(f, first_wave)
    else:
        by_clip = []
    for copy in later[len(by_clip):]:
        copy.wait_recv()
    for f in range(frames):
        latent = projected(f, last_wave)
        if last_wave is not None:
            latent = latent + total_ref[f]
        latent = latent.astype(jnp.bfloat16).astype(jnp.float32)
        for c in range(0, columns, LANES):
            value = latent[:, c:c + LANES]
            square = value * value
            high = square.astype(jnp.bfloat16)
            low = (square - high.astype(jnp.float32)).astype(jnp.bfloat16)
            total = jnp.dot(
                jnp.concatenate([high, low], axis=1), same, preferred_element_type=jnp.float32)
            scaled = value * lax.rsqrt(total * (1.0 / IDM_DIM) + 1e-6) * gain_ref[:, c:c + LANES]
            out_ref[f, :, c:c + LANES] = scaled.astype(out_ref.dtype)

    for copy in started + later + exchanged:
        copy.wait_send()
    for hop, copy in count_copies:
        pl.when(tm + hop < n)(copy.wait_send)
    for group in firsts + relays:
        for entry in group:
            pl.when(entry[1])(entry[0].wait_send)


def normed_latent(mesh, queries, keyvals, proj_weight, norm_gain, frame_counts):
    n, clips, tiles = (mesh.shape[a] for a in ("tm", "clip", "tile"))
    frames, tokens, width = queries.shape
    rows, columns = proj_weight.shape
    plan = halo_plan(frames)
    hops = len(plan)
    rest = max(1, plan[0][1] - plan[1][1]) if hops > 1 else 1
    roles = max(6, hops) * KVHEADS
    steps = max(1, n // 2)
    units = frames * KVHEADS
    dma = pltpu.SemaphoreType.DMA
    hbm = pl.BlockSpec(memory_space=pltpu.HBM)
    vmem = pl.BlockSpec(memory_space=pltpu.VMEM)
    bf16 = jnp.bfloat16
    flops = frames * tokens * width * 4 * WINDOW * tokens + 2 * frames * tiles * tokens * width * columns
    return pl.pallas_call(
        functools.partial(latent_kernel, n, clips, tiles, columns_of(mesh)),
        out_shape=jax.ShapeDtypeStruct((frames, tiles * tokens, columns), bf16),
        in_specs=[pl.BlockSpec(memory_space=pltpu.SMEM), hbm, hbm, hbm, vmem],
        out_specs=vmem,
        scratch_shapes=[
            pltpu.VMEM(queries.shape, bf16),
            pltpu.VMEM((2, LEAD + frames) + keyvals.shape[2:], bf16),
            pltpu.VMEM((2, rest) + keyvals.shape[2:], bf16),
            pltpu.VMEM((n, rows, columns), bf16),
            pltpu.VMEM((frames, tiles, tokens, width), bf16),
            pltpu.VMEM((frames, tiles * tokens, columns), jnp.float32),
            pltpu.VMEM((hops + 1, max(8, frames), LANES), jnp.int32),
            pltpu.VMEM((LEAD + frames, tokens, LANES), bf16),
            dma((3,)), dma((roles,)), dma((roles,)), dma((hops,)), dma((hops,)),
            dma((4 * steps,)), dma((4 * steps,)), dma((4 * steps,)), dma((4 * steps,)),
            dma((units,)), dma((units,)),
        ],
        compiler_params=pltpu.CompilerParams(
            collective_id=0, has_side_effects=True, vmem_limit_bytes=60 * 2 ** 20),
        cost_estimate=pl.CostEstimate(
            flops=flops, bytes_accessed=8 * 2 ** 20, transcendentals=0),
    )(frame_counts, queries, keyvals, proj_weight, norm_gain.reshape(1, -1))


def partner_kernel(sources, counts_ref, *refs):
    out_ref = refs[-1]
    frame = pl.program_id(0)
    tokens, columns = out_ref.shape[1:]
    keys = sources * tokens
    slots = lax.broadcasted_iota(jnp.int32, (tokens, LANES), 0)
    live = jnp.concatenate(
        [slots < counts_ref[source, frame] for source in range(sources)], axis=0)
    lower = lax.broadcasted_iota(jnp.int32, (tokens, LANES), 1) < IDM_DIM
    scale = IDM_DIM ** (-0.5) * LOG2E
    for c in range(0, columns, LANES):
        k = jnp.concatenate([ref[0, :, c:c + LANES] for ref in refs[:sources]], axis=0)
        q = refs[0][0, :, c:c + LANES]
        zero = jnp.zeros_like(q)
        q = jnp.concatenate([jnp.where(lower, q, zero), jnp.where(lower, zero, q)], axis=0)
        v = jnp.concatenate(
            [jnp.where(live, k, jnp.zeros_like(k)), live.astype(k.dtype)], axis=1)
        scores = lax.dot_general(q, k, (((1,), (1,)), ((), ())), preferred_element_type=jnp.float32)
        weights = jnp.exp2(scores * scale).astype(jnp.bfloat16)
        mixed = jnp.dot(weights, v, preferred_element_type=jnp.float32)
        result = mixed[:, :LANES] / mixed[:, LANES:]
        out_ref[0, :, c:c + LANES] = jnp.where(
            lower, result[:tokens], result[tokens:]).astype(out_ref.dtype)


def partner_attention(counts, blocks):
    frames, tokens, columns = blocks[0].shape
    spec = pl.BlockSpec((1, tokens, columns), lambda f: (f, 0, 0))
    return pl.pallas_call(
        functools.partial(partner_kernel, len(blocks)),
        out_shape=jax.ShapeDtypeStruct(blocks[0].shape, jnp.bfloat16),
        grid=(frames,),
        in_specs=[pl.BlockSpec(memory_space=pltpu.SMEM)] + [spec] * len(blocks),
        out_specs=spec,
        compiler_params=pltpu.CompilerParams(vmem_limit_bytes=60 * 2 ** 20),
    )(counts, *blocks)


def local(mesh, queries, keyvals, proj_weight, norm_gain, frame_counts):
    normed = normed_latent(mesh, queries, keyvals, proj_weight, norm_gain, frame_counts)
    distance = PARTNER // queries.shape[0]
    blocks, counts = [normed], [frame_counts]
    for steps in (distance, -distance):
        if distance < mesh.shape["tm"]:
            block, count = passed_along((normed, frame_counts), "tm", steps)
            blocks.append(block)
            counts.append(count)
    return partner_attention(jnp.stack(counts), blocks)


def solution(mesh):
    in_specs = (
        P(("clip", "tm"), "tile", None),
        P(None, ("clip", "tm"), "tile", None),
        P("tm", "tile"),
        P("tile"),
        P(("clip", "tm")),
    )
    out_specs = P(("clip", "tm"), None, "tile")
    return jax.shard_map(
        functools.partial(local, mesh), mesh=mesh, in_specs=in_specs, out_specs=out_specs,
        check_vma=False)
```

```python
import functools
import math

import jax
import jax.numpy as jnp
from jax import lax
from jax.experimental import pallas as pl
from jax.experimental.pallas import tpu as pltpu
from jax.sharding import PartitionSpec as P

QHEADS = 16
KVHEADS = 4
HEAD_DIM = 128
IDM_DIM = 64
WINDOW = 4
PARTNER = 16
LEAD = WINDOW - 1
LANES = 128
TILE_ROWS = 16
DEAD = -1e30
LOG2E = math.log2(math.e)
MESH = pl.DeviceIdType.MESH


def passed_along(value, axis, steps):
    count = lax.axis_size(axis)
    initial, last = (max(0, -steps), min(count, count - steps))
    return lax.ppermute(value, axis, [(source, source + steps) for source in range(initial, last)])


def columns_of(mesh):
    place = mesh.axis_names.index("tm")
    line = mesh.devices.transpose(
        [place] + [i for i in range(mesh.devices.ndim) if i != place]
    ).reshape(mesh.shape["tm"], -1)[:, 0]
    coords = [getattr(device, "coords", None) for device in line]
    if coords[0] is None or len(line) == 1:
        return 1
    moved = [i for i in range(len(coords[0])) if coords[0][i] != coords[1][i]]
    if len(moved) != 1:
        return 1
    columns = len({c[moved[0]] for c in coords})
    return columns if len(line) % columns == 0 else 1


def halo_plan(frames):
    plan, covered, hop = [], 0, 1
    while covered < LEAD:
        needed = min(frames, LEAD - covered)
        covered += needed
        plan.append((hop, needed, LEAD - covered))
        hop += 1
    return plan


def relayed(plan, x_count, n):
    return x_count == 2 and n % 2 == 0 and len(plan) == 2 and plan[0][1] > plan[1][1]


def ring_chunks(rows, clip, clips):
    over = rows * 7 // 16 // TILE_ROWS * TILE_ROWS if clips == 2 else 0
    ahead = -(-over // 2 // TILE_ROWS) * TILE_ROWS
    if not over or ahead == over:
        half = rows // 2 // TILE_ROWS * TILE_ROWS
        return [(at, size, 0, 0) for at, size in ((0, half), (half, rows - half)) if size]
    first = clip * (rows - ahead)
    return [
        (first, ahead, first, ahead),
        (ahead + clip * (over - ahead), rows - over - ahead,
         ahead + clip * (rows - over - ahead), over - ahead),
    ]


def latent_kernel(
    n, clips, tiles, x_count,
    counts_ref, q_ref, kv_ref, w_ref, gain_ref, out_ref,
    q_buf, kv_win, stash, w_full, att, total_ref, counts, bias,
    local_sem, halo_send, halo_recv, count_send, count_recv,
    ring_send, ring_recv, clip_send, clip_recv, tile_send, tile_recv,
):
    clip, tm, tile = lax.axis_index("clip"), lax.axis_index("tm"), lax.axis_index("tile")
    frames, tokens, width = q_ref.shape
    rows = w_ref.shape[0]
    groups = QHEADS // KVHEADS
    plan = halo_plan(frames)
    z_count = n // x_count

    def place_of(index):
        x, z = lax.rem(index, x_count), index // x_count
        return x * z_count + z + lax.rem(x, 2) * (z_count - 1 - 2 * z)

    def index_of(place):
        place = lax.rem(place + 2 * n, n)
        x, z = place // z_count, lax.rem(place, z_count)
        return (z + lax.rem(x, 2) * (z_count - 1 - 2 * z)) * x_count + x

    place = place_of(tm)
    ends = (index_of(place + 1), index_of(place - 1))

    own_copies = [
        pltpu.make_async_copy(kv_ref, kv_win.at[:, LEAD:LEAD + frames], local_sem.at[0]),
        pltpu.make_async_copy(q_ref, q_buf, local_sem.at[1]),
        pltpu.make_async_copy(w_ref, w_full.at[tm], local_sem.at[2]),
    ]
    for copy in own_copies:
        copy.start()

    barrier = pltpu.get_barrier_semaphore()
    expected = 0
    if n > 1:
        for end in ends:
            pl.semaphore_signal(barrier, inc=1, device_id={"tm": end}, device_id_type=MESH)
            expected += 1
    if clips == 2:
        pl.semaphore_signal(barrier, inc=1, device_id={"clip": 1 - clip}, device_id_type=MESH)
        expected += 1
    if tiles == 2:
        pl.semaphore_signal(barrier, inc=1, device_id={"tile": 1 - tile}, device_id_type=MESH)
        expected += 1
    for hop, _, _ in plan:
        @pl.when(tm + hop < n)
        def _():
            pl.semaphore_signal(barrier, inc=1, device_id={"tm": tm + hop}, device_id_type=MESH)

        @pl.when(tm >= hop)
        def _():
            pl.semaphore_signal(barrier, inc=1, device_id={"tm": tm - hop}, device_id_type=MESH)

        expected = expected + jnp.where(tm + hop < n, 1, 0) + jnp.where(tm >= hop, 1, 0)
    for f in range(frames):
        counts[0, f:f + 1, :] = jnp.full((1, LANES), counts_ref[f], jnp.int32)
    pl.semaphore_wait(barrier, expected)

    count_copies = []
    for i, (hop, _, _) in enumerate(plan):
        count_copies.append((hop, pltpu.make_async_remote_copy(
            src_ref=counts.at[0], dst_ref=counts.at[hop],
            send_sem=count_send.at[i], recv_sem=count_recv.at[i],
            device_id={"tm": lax.rem(tm + hop, n)}, device_id_type=MESH)))
    for hop, copy in count_copies:
        pl.when(tm + hop < n)(copy.start)

    def halo_copy(role, arrival, g, source, first, count, place_at, hop):
        span = pl.ds(g * HEAD_DIM, HEAD_DIM)
        target = stash if place_at is None else kv_win.at[:, place_at:place_at + count]
        return pltpu.make_async_remote_copy(
            src_ref=source.at[:, first:first + count, :, span],
            dst_ref=target.at[:, :, :, span],
            send_sem=halo_send.at[role * KVHEADS + g],
            recv_sem=halo_recv.at[arrival * KVHEADS + g],
            device_id={"tm": lax.rem(tm + hop + n, n)}, device_id_type=MESH)

    firsts, relays, arrivals = [[] for _ in range(KVHEADS)], [], []
    if relayed(plan, x_count, n):
        (_, needed, start), (_, last, start2) = plan
        rest = needed - last
        even, odd = lax.rem(tm, 2) == 0, lax.rem(tm, 2) == 1
        up, down = tm + 2 < n, tm >= 2
        for g in range(KVHEADS):
            firsts[g] += [
                (halo_copy(2, 2, g, kv_ref, frames - last, last, start2, 2), up),
                (halo_copy(3, 3, g, kv_ref, frames - needed, rest, None, -1),
                 jnp.logical_and(odd, up)),
                (halo_copy(0, 0, g, kv_ref, frames - needed, rest, start, 1), even),
                (halo_copy(1, 1, g, kv_ref, frames - last, last, start + rest, 1), even),
            ]
            relays.append([
                (halo_copy(4, 0, g, stash, 0, rest, start, 2), jnp.logical_and(even, up), 3),
                (halo_copy(5, 1, g, kv_win, start2, last, start + rest, -1),
                 jnp.logical_and(odd, down), 2),
            ])
            arrivals.append([
                (0, tm >= 1, rest, start), (1, tm >= 1, last, start + rest),
                (2, jnp.logical_and(even, down), last, start2),
            ])
    else:
        for g in range(KVHEADS):
            for i, (hop, needed, start) in enumerate(plan):
                firsts[g].append((
                    halo_copy(i, i, g, kv_ref, frames - needed, needed, start, hop), tm + hop < n))
            relays.append([])
            arrivals.append([
                (i, tm >= hop, needed, start) for i, (hop, needed, start) in enumerate(plan)])

    def issue(g):
        if g < KVHEADS:
            for copy, mine in firsts[g]:
                pl.when(mine)(copy.start)

    def arrival_of(arrival, g, count, place_at):
        return halo_copy(0, arrival, g, kv_ref, 0, count, place_at, 1)

    def relay(g):
        for copy, mine, arrival in relays[g]:
            @pl.when(mine)
            def _():
                count, place_at = (rest, None) if arrival == 3 else (last, start2)
                arrival_of(arrival, g, count, place_at).wait_recv()
                copy.start()

    def arrive(g):
        for arrival, mine, count, place_at in arrivals[g]:
            pl.when(mine)(arrival_of(arrival, g, count, place_at).wait_recv)

    chunks = ring_chunks(rows, clip, clips)
    steps = n // 2
    started, later = [], []

    def ring_copy(way, step, c):
        start, size, _, _ = chunks[c]
        owner = index_of(place - step * (1 - 2 * way))
        span = pl.ds(start if isinstance(start, int) else pl.multiple_of(start, TILE_ROWS), size)
        slot = (way * max(steps, 1) + step) * len(chunks) + c
        return pltpu.make_async_remote_copy(
            src_ref=w_ref.at[span] if step == 0 else w_full.at[owner, span],
            dst_ref=w_full.at[owner, span],
            send_sem=ring_send.at[slot], recv_sem=ring_recv.at[slot],
            device_id={"tm": ends[way]}, device_id_type=MESH)

    def goes(way, step, c):
        return n % 2 == 1 or step < steps - 1 or c % 2 == way

    def send_step(way, step, c):
        if step < steps and goes(way, step, c):
            copy = ring_copy(way, step, c)
            copy.start()
            started.append(copy)

    def take(step, c):
        if c < len(chunks):
            for way in range(2):
                if not goes(way, step, c):
                    continue
                ring_copy(way, step, c).wait_recv()
                send_step(way, step + 1, c)
                _, _, start, size = chunks[c]
                if size:
                    owner = index_of(place - (step + 1) * (1 - 2 * way))
                    span = pl.ds(pl.multiple_of(start, TILE_ROWS), size)
                    slot = (way * steps + step) * len(chunks) + c
                    copy = pltpu.make_async_remote_copy(
                        src_ref=w_full.at[owner, span], dst_ref=w_full.at[owner, span],
                        send_sem=clip_send.at[slot], recv_sem=clip_recv.at[slot],
                        device_id={"clip": 1 - clip}, device_id_type=MESH)
                    copy.start()
                    later.append(copy)

    for c in range(len(chunks)):
        for way in range(2):
            send_step(way, 0, c)
        if c == 0:
            issue(0)
    issue(1)

    for hop, needed, start in plan:
        @pl.when(tm < hop)
        def _():
            counts[hop] = jnp.zeros(counts.shape[1:], jnp.int32)
            kv_win[:, start:start + needed] = jnp.zeros(
                (2, needed) + kv_win.shape[2:], kv_win.dtype)

    for hop, copy in count_copies:
        pl.when(tm >= hop)(copy.wait_recv)
    own_copies[0].wait()
    own_copies[1].wait()

    slots = tile * tokens + lax.broadcasted_iota(jnp.int32, (tokens, LANES), 0)
    first_lane = lax.broadcasted_iota(jnp.int32, (tokens, LANES), 1) == 0
    for w in range(LEAD + frames):
        if w >= LEAD:
            row = counts[0, w - LEAD:w - LEAD + 1, :]
        else:
            hop, needed, start = [p for p in plan if p[2] <= w < p[2] + p[1]][0]
            at = frames - needed + w - start
            row = counts[hop, at:at + 1, :]
        bias[w] = jnp.where(
            jnp.logical_and(first_lane, slots >= row), DEAD, 0.0).astype(bias.dtype)

    keys = WINDOW * tokens
    unit_lane = (
        lax.broadcasted_iota(jnp.int32, (groups * tokens, LANES), 1) == 0
    ).astype(jnp.bfloat16)
    ones = jnp.ones((keys, LANES), jnp.bfloat16)
    scale = HEAD_DIM ** (-0.5) * LOG2E
    exchanged = []
    taken = 0
    relay(0)
    for unit in range(KVHEADS * frames):
        g, f = unit // frames, unit % frames
        if f == 0:
            if taken < steps - 1:
                take(taken, 0)
            issue(g + 2)
            arrive(g)
        if f == frames - 1:
            if taken < steps - 1:
                take(taken, 1)
                taken += 1
            if g + 1 < KVHEADS:
                relay(g + 1)
        span = slice(g * HEAD_DIM, (g + 1) * HEAD_DIM)
        k = kv_win[0, f:f + WINDOW, :, span].reshape(keys, HEAD_DIM)
        v = kv_win[1, f:f + WINDOW, :, span].reshape(keys, HEAD_DIM)
        k = jnp.concatenate([k, bias[f:f + WINDOW].reshape(keys, LANES)], axis=1)
        v = jnp.concatenate([v, ones], axis=1)
        q = jnp.concatenate(
            [q_buf[f, :, (g * groups + i) * HEAD_DIM:(g * groups + i + 1) * HEAD_DIM]
             for i in range(groups)], axis=0)
        q = jnp.concatenate([q, unit_lane], axis=1)
        scores = lax.dot_general(q, k, (((1,), (1,)), ((), ())), preferred_element_type=jnp.float32)
        top = jnp.max(scores, axis=-1, keepdims=True)
        weights = jnp.exp2((scores - top) * scale).astype(jnp.bfloat16)
        mixed = jnp.dot(weights, v, preferred_element_type=jnp.float32)
        result = (mixed[:, :HEAD_DIM] / mixed[:, HEAD_DIM:]).astype(jnp.bfloat16)
        for i in range(groups):
            at = (g * groups + i) * HEAD_DIM
            att[f, tile, :, at:at + HEAD_DIM] = result[i * tokens:(i + 1) * tokens]
        if tiles == 2:
            part = att.at[f, tile, :, g * groups * HEAD_DIM:(g + 1) * groups * HEAD_DIM]
            copy = pltpu.make_async_remote_copy(
                src_ref=part, dst_ref=part,
                send_sem=tile_send.at[unit], recv_sem=tile_recv.at[unit],
                device_id={"tile": 1 - tile}, device_id_type=MESH)
            copy.start()
            exchanged.append(copy)
    while taken < steps:
        before_last = list(later)
        take(taken, 0)
        take(taken, 1)
        taken += 1

    columns = w_ref.shape[1]
    same = (
        lax.rem(lax.broadcasted_iota(jnp.int32, (2 * LANES, LANES), 0), LANES) // IDM_DIM
        == lax.broadcasted_iota(jnp.int32, (2 * LANES, LANES), 1) // IDM_DIM
    ).astype(jnp.bfloat16)
    own_copies[2].wait()
    for copy in exchanged:
        copy.wait_recv()

    def projected(f, owners):
        if owners is None:
            return jnp.dot(
                att[f].reshape(tiles * tokens, width), w_full[...].reshape(n * rows, columns),
                preferred_element_type=jnp.float32)
        parts = []
        for owner in owners:
            span = pl.ds(pl.multiple_of(owner * rows, LANES), rows)
            parts.append(jnp.dot(
                att[f, :, :, span].reshape(tiles * tokens, rows), w_full[owner],
                preferred_element_type=jnp.float32))
        return sum(parts)

    first_wave, last_wave = [tm], None
    by_clip = before_last if steps else []
    if rows % LANES == 0 and steps > 1:
        for step in range(steps - 1):
            first_wave += [index_of(place - step - 1), index_of(place + step + 1)]
        last_wave = [index_of(place - steps)]
        if n % 2:
            last_wave.append(index_of(place + steps))
        for copy in by_clip:
            copy.wait_recv()
        for f in range(frames):
            total_ref[f] = projected(f, first_wave)
    else:
        by_clip = []
    for copy in later[len(by_clip):]:
        copy.wait_recv()
    for f in range(frames):
        latent = projected(f, last_wave)
        if last_wave is not None:
            latent = latent + total_ref[f]
        latent = latent.astype(jnp.bfloat16).astype(jnp.float32)
        for c in range(0, columns, LANES):
            value = latent[:, c:c + LANES]
            square = value * value
            high = square.astype(jnp.bfloat16)
            low = (square - high.astype(jnp.float32)).astype(jnp.bfloat16)
            total = jnp.dot(
                jnp.concatenate([high, low], axis=1), same, preferred_element_type=jnp.float32)
            scaled = value * lax.rsqrt(total * (1.0 / IDM_DIM) + 1e-6) * gain_ref[:, c:c + LANES]
            out_ref[f, :, c:c + LANES] = scaled.astype(out_ref.dtype)

    for copy in started + later + exchanged:
        copy.wait_send()
    for hop, copy in count_copies:
        pl.when(tm + hop < n)(copy.wait_send)
    for group in firsts + relays:
        for entry in group:
            pl.when(entry[1])(entry[0].wait_send)


def normed_latent(mesh, queries, keyvals, proj_weight, norm_gain, frame_counts):
    n, clips, tiles = (mesh.shape[a] for a in ("tm", "clip", "tile"))
    frames, tokens, width = queries.shape
    rows, columns = proj_weight.shape
    plan = halo_plan(frames)
    hops = len(plan)
    rest = max(1, plan[0][1] - plan[1][1]) if hops > 1 else 1
    roles = max(6, hops) * KVHEADS
    steps = max(1, n // 2)
    units = frames * KVHEADS
    dma = pltpu.SemaphoreType.DMA
    hbm = pl.BlockSpec(memory_space=pltpu.HBM)
    vmem = pl.BlockSpec(memory_space=pltpu.VMEM)
    bf16 = jnp.bfloat16
    flops = frames * tokens * width * 4 * WINDOW * tokens + 2 * frames * tiles * tokens * width * columns
    return pl.pallas_call(
        functools.partial(latent_kernel, n, clips, tiles, columns_of(mesh)),
        out_shape=jax.ShapeDtypeStruct((frames, tiles * tokens, columns), bf16),
        in_specs=[pl.BlockSpec(memory_space=pltpu.SMEM), hbm, hbm, hbm, vmem],
        out_specs=vmem,
        scratch_shapes=[
            pltpu.VMEM(queries.shape, bf16),
            pltpu.VMEM((2, LEAD + frames) + keyvals.shape[2:], bf16),
            pltpu.VMEM((2, rest) + keyvals.shape[2:], bf16),
            pltpu.VMEM((n, rows, columns), bf16),
            pltpu.VMEM((frames, tiles, tokens, width), bf16),
            pltpu.VMEM((frames, tiles * tokens, columns), jnp.float32),
            pltpu.VMEM((hops + 1, max(8, frames), LANES), jnp.int32),
            pltpu.VMEM((LEAD + frames, tokens, LANES), bf16),
            dma((3,)), dma((roles,)), dma((roles,)), dma((hops,)), dma((hops,)),
            dma((4 * steps,)), dma((4 * steps,)), dma((4 * steps,)), dma((4 * steps,)),
            dma((units,)), dma((units,)),
        ],
        compiler_params=pltpu.CompilerParams(
            collective_id=0, has_side_effects=True, vmem_limit_bytes=60 * 2 ** 20),
        cost_estimate=pl.CostEstimate(
            flops=flops, bytes_accessed=8 * 2 ** 20, transcendentals=0),
    )(frame_counts, queries, keyvals, proj_weight, norm_gain.reshape(1, -1))


def partner_kernel(sources, counts_ref, *refs):
    out_ref = refs[-1]
    frame = pl.program_id(0)
    tokens, columns = out_ref.shape[1:]
    keys = sources * tokens
    slots = lax.broadcasted_iota(jnp.int32, (tokens, LANES), 0)
    live = jnp.concatenate(
        [slots < counts_ref[source, frame] for source in range(sources)], axis=0)
    lower = lax.broadcasted_iota(jnp.int32, (tokens, LANES), 1) < IDM_DIM
    scale = IDM_DIM ** (-0.5) * LOG2E
    for c in range(0, columns, LANES):
        k = jnp.concatenate([ref[0, :, c:c + LANES] for ref in refs[:sources]], axis=0)
        q = refs[0][0, :, c:c + LANES]
        zero = jnp.zeros_like(q)
        q = jnp.concatenate([jnp.where(lower, q, zero), jnp.where(lower, zero, q)], axis=0)
        v = jnp.concatenate(
            [jnp.where(live, k, jnp.zeros_like(k)), live.astype(k.dtype)], axis=1)
        scores = lax.dot_general(q, k, (((1,), (1,)), ((), ())), preferred_element_type=jnp.float32)
        weights = jnp.exp2(scores * scale).astype(jnp.bfloat16)
        mixed = jnp.dot(weights, v, preferred_element_type=jnp.float32)
        total = jnp.where(lower, mixed[:tokens, LANES:], mixed[tokens:, LANES:])
        result = jnp.where(lower, mixed[:tokens, :LANES], mixed[tokens:, :LANES]) / total
        out_ref[0, :, c:c + LANES] = result.astype(out_ref.dtype)


def partner_attention(counts, blocks):
    frames, tokens, columns = blocks[0].shape
    spec = pl.BlockSpec((1, tokens, columns), lambda f: (f, 0, 0))
    return pl.pallas_call(
        functools.partial(partner_kernel, len(blocks)),
        out_shape=jax.ShapeDtypeStruct(blocks[0].shape, jnp.bfloat16),
        grid=(frames,),
        in_specs=[pl.BlockSpec(memory_space=pltpu.SMEM)] + [spec] * len(blocks),
        out_specs=spec,
        compiler_params=pltpu.CompilerParams(vmem_limit_bytes=60 * 2 ** 20),
    )(counts, *blocks)


def local(mesh, queries, keyvals, proj_weight, norm_gain, frame_counts):
    normed = normed_latent(mesh, queries, keyvals, proj_weight, norm_gain, frame_counts)
    distance = PARTNER // queries.shape[0]
    blocks, counts = [normed], [frame_counts]
    for steps in (distance, -distance):
        if distance < mesh.shape["tm"]:
            block, count = passed_along((normed, frame_counts), "tm", steps)
            blocks.append(block)
            counts.append(count)
    return partner_attention(jnp.stack(counts), blocks)


def solution(mesh):
    in_specs = (
        P(("clip", "tm"), "tile", None),
        P(None, ("clip", "tm"), "tile", None),
        P("tm", "tile"),
        P("tile"),
        P(("clip", "tm")),
    )
    out_specs = P(("clip", "tm"), None, "tile")
    return jax.shard_map(
        functools.partial(local, mesh), mesh=mesh, in_specs=in_specs, out_specs=out_specs,
        check_vma=False)
```

```python
import functools
import math

import jax
import jax.numpy as jnp
from jax import lax
from jax.experimental import pallas as pl
from jax.experimental.pallas import tpu as pltpu
from jax.sharding import PartitionSpec as P

QHEADS = 16
KVHEADS = 4
HEAD_DIM = 128
IDM_DIM = 64
WINDOW = 4
PARTNER = 16
LEAD = WINDOW - 1
LANES = 128
TILE_ROWS = 16
DEAD = -1e30
LOG2E = math.log2(math.e)
MESH = pl.DeviceIdType.MESH


def passed_along(value, axis, steps):
    count = lax.axis_size(axis)
    initial, last = (max(0, -steps), min(count, count - steps))
    return lax.ppermute(value, axis, [(source, source + steps) for source in range(initial, last)])


def columns_of(mesh):
    place = mesh.axis_names.index("tm")
    line = mesh.devices.transpose(
        [place] + [i for i in range(mesh.devices.ndim) if i != place]
    ).reshape(mesh.shape["tm"], -1)[:, 0]
    coords = [getattr(device, "coords", None) for device in line]
    if coords[0] is None or len(line) == 1:
        return 1
    moved = [i for i in range(len(coords[0])) if coords[0][i] != coords[1][i]]
    if len(moved) != 1:
        return 1
    columns = len({c[moved[0]] for c in coords})
    return columns if len(line) % columns == 0 else 1


def halo_plan(frames):
    plan, covered, hop = [], 0, 1
    while covered < LEAD:
        needed = min(frames, LEAD - covered)
        covered += needed
        plan.append((hop, needed, LEAD - covered))
        hop += 1
    return plan


def relayed(plan, x_count, n):
    return x_count == 2 and n % 2 == 0 and len(plan) == 2 and plan[0][1] > plan[1][1]


def ring_chunks(rows, clip, clips):
    over = clips == 2 and rows % (2 * TILE_ROWS) == 0
    start, size = (clip * (rows // 2), rows // 2) if over else (0, rows)
    pieces = 4
    while size % (pieces * TILE_ROWS):
        pieces //= 2
        if pieces <= 1:
            return [(start, size, over)]
    size //= pieces
    return [(start + i * size, size, over) for i in range(pieces)]


def latent_kernel(
    n, clips, tiles, x_count,
    counts_ref, q_ref, kv_ref, w_ref, gain_ref, out_ref,
    q_buf, kv_win, stash, w_full, att, total_ref, counts, bias,
    local_sem, halo_send, halo_recv, count_send, count_recv,
    ring_send, ring_recv, clip_send, clip_recv, tile_send, tile_recv,
):
    clip, tm, tile = lax.axis_index("clip"), lax.axis_index("tm"), lax.axis_index("tile")
    frames, tokens, width = q_ref.shape
    rows = w_ref.shape[0]
    groups = QHEADS // KVHEADS
    plan = halo_plan(frames)
    z_count = n // x_count

    def place_of(index):
        x, z = lax.rem(index, x_count), index // x_count
        return x * z_count + z + lax.rem(x, 2) * (z_count - 1 - 2 * z)

    def index_of(place):
        place = lax.rem(place + 2 * n, n)
        x, z = place // z_count, lax.rem(place, z_count)
        return (z + lax.rem(x, 2) * (z_count - 1 - 2 * z)) * x_count + x

    place = place_of(tm)
    ends = (index_of(place + 1), index_of(place - 1))

    own_copies = [
        pltpu.make_async_copy(kv_ref, kv_win.at[:, LEAD:LEAD + frames], local_sem.at[0]),
        pltpu.make_async_copy(q_ref, q_buf, local_sem.at[1]),
        pltpu.make_async_copy(w_ref, w_full.at[tm], local_sem.at[2]),
    ]
    for copy in own_copies:
        copy.start()

    barrier = pltpu.get_barrier_semaphore()
    expected = 0
    if n > 1:
        for end in ends:
            pl.semaphore_signal(barrier, inc=1, device_id={"tm": end}, device_id_type=MESH)
            expected += 1
    if clips == 2:
        pl.semaphore_signal(barrier, inc=1, device_id={"clip": 1 - clip}, device_id_type=MESH)
        expected += 1
    if tiles == 2:
        pl.semaphore_signal(barrier, inc=1, device_id={"tile": 1 - tile}, device_id_type=MESH)
        expected += 1
    for hop, _, _ in plan:
        @pl.when(tm + hop < n)
        def _():
            pl.semaphore_signal(barrier, inc=1, device_id={"tm": tm + hop}, device_id_type=MESH)

        @pl.when(tm >= hop)
        def _():
            pl.semaphore_signal(barrier, inc=1, device_id={"tm": tm - hop}, device_id_type=MESH)

        expected = expected + jnp.where(tm + hop < n, 1, 0) + jnp.where(tm >= hop, 1, 0)
    for f in range(frames):
        counts[0, f:f + 1, :] = jnp.full((1, LANES), counts_ref[f], jnp.int32)
    pl.semaphore_wait(barrier, expected)

    count_copies = []
    for i, (hop, _, _) in enumerate(plan):
        count_copies.append((hop, pltpu.make_async_remote_copy(
            src_ref=counts.at[0], dst_ref=counts.at[hop],
            send_sem=count_send.at[i], recv_sem=count_recv.at[i],
            device_id={"tm": lax.rem(tm + hop, n)}, device_id_type=MESH)))
    for hop, copy in count_copies:
        pl.when(tm + hop < n)(copy.start)

    def halo_copy(role, arrival, g, source, first, count, place_at, hop, pair=(0, 2)):
        span = pl.ds(g * HEAD_DIM, HEAD_DIM)
        taken_from = pair if source is not stash else (0, 1)
        target = stash if place_at is None else kv_win.at[
            pair[0]:pair[1], place_at:place_at + count]
        return pltpu.make_async_remote_copy(
            src_ref=source.at[taken_from[0]:taken_from[1], first:first + count, :, span],
            dst_ref=target.at[:, :, :, span],
            send_sem=halo_send.at[role * KVHEADS + g],
            recv_sem=halo_recv.at[arrival * KVHEADS + g],
            device_id={"tm": lax.rem(tm + hop + n, n)}, device_id_type=MESH)

    firsts, relays, arrivals = [[] for _ in range(KVHEADS)], [], []
    if relayed(plan, x_count, n):
        (_, needed, start), (_, last, start2) = plan
        rest = needed - last
        even, odd = lax.rem(tm, 2) == 0, lax.rem(tm, 2) == 1
        up, down = tm + 2 < n, tm >= 2
        for g in range(KVHEADS):
            firsts[g] += [
                (halo_copy(2, 2, g, kv_ref, frames - last, last, start2, 2), up),
                (halo_copy(3, 3, g, kv_ref, frames - needed, rest, None, -1, (0, 1)),
                 jnp.logical_and(odd, up)),
                (halo_copy(6, 3, g, kv_ref, frames - needed, rest, None, 2, (1, 2)),
                 jnp.logical_and(odd, up)),
                (halo_copy(0, 0, g, kv_ref, frames - needed, rest, start, 1), even),
                (halo_copy(1, 1, g, kv_ref, frames - last, last, start + rest, 1), even),
            ]
            keys_part, values_part = (0, 1), (1, 2)
            relays.append([
                (halo_copy(4, 0, g, stash, 0, rest, start, 2, keys_part),
                 jnp.logical_and(even, up), (3, g, rest, None, keys_part)),
                (halo_copy(7, 6, g, stash, 0, rest, start, -1, values_part),
                 jnp.logical_and(odd, down), (3, g, rest, None, values_part)),
                (halo_copy(5, 1, g, kv_win, start2, last, start + rest, -1),
                 jnp.logical_and(odd, down), (2, g, last, start2)),
            ])
            arrivals.append([
                ((0, g, rest, start), odd),
                ((0, g, rest, start, keys_part), jnp.logical_and(even, down)),
                ((6, g, rest, start, values_part), jnp.logical_and(even, down)),
                ((1, g, last, start + rest), tm >= 1),
                ((2, g, last, start2), jnp.logical_and(even, down)),
            ])
    else:
        for g in range(KVHEADS):
            for i, (hop, needed, start) in enumerate(plan):
                firsts[g].append((
                    halo_copy(i, i, g, kv_ref, frames - needed, needed, start, hop), tm + hop < n))
            relays.append([])
            arrivals.append([
                ((i, g, needed, start), tm >= hop) for i, (hop, needed, start) in enumerate(plan)])

    def issue(g):
        if g < KVHEADS:
            for copy, mine in firsts[g]:
                pl.when(mine)(copy.start)

    def arrival_of(arrival, g, count, place_at, pair=(0, 2)):
        return halo_copy(0, arrival, g, kv_ref, 0, count, place_at, 1, pair)

    def relay(g):
        for copy, mine, arrival in relays[g]:
            @pl.when(mine)
            def _():
                arrival_of(*arrival).wait_recv()
                copy.start()

    def arrive(g):
        for arrival, mine in arrivals[g]:
            pl.when(mine)(arrival_of(*arrival).wait_recv)

    chunks = ring_chunks(rows, clip, clips)
    steps = n // 2
    started, later = [], []

    def ring_copy(way, step, c):
        start, size, _ = chunks[c]
        owner = index_of(place - step * (1 - 2 * way))
        span = pl.ds(start if isinstance(start, int) else pl.multiple_of(start, TILE_ROWS), size)
        slot = (way * max(steps, 1) + step) * len(chunks) + c
        return pltpu.make_async_remote_copy(
            src_ref=w_ref.at[span] if step == 0 else w_full.at[owner, span],
            dst_ref=w_full.at[owner, span],
            send_sem=ring_send.at[slot], recv_sem=ring_recv.at[slot],
            device_id={"tm": ends[way]}, device_id_type=MESH)

    def goes(way, step, c):
        return n % 2 == 1 or step < steps - 1 or c % 2 == way

    def send_step(way, step, c):
        if step < steps and goes(way, step, c):
            copy = ring_copy(way, step, c)
            copy.start()
            started.append(copy)

    def take(step, part):
        half = (len(chunks) + 1) // 2
        for c in range(part * half, min(len(chunks), part * half + half)):
            for way in range(2):
                if not goes(way, step, c):
                    continue
                ring_copy(way, step, c).wait_recv()
                send_step(way, step + 1, c)
                start, size, over = chunks[c]
                if over:
                    owner = index_of(place - (step + 1) * (1 - 2 * way))
                    span = pl.ds(pl.multiple_of(start, TILE_ROWS), size)
                    slot = (way * steps + step) * len(chunks) + c
                    copy = pltpu.make_async_remote_copy(
                        src_ref=w_full.at[owner, span], dst_ref=w_full.at[owner, span],
                        send_sem=clip_send.at[slot], recv_sem=clip_recv.at[slot],
                        device_id={"clip": 1 - clip}, device_id_type=MESH)
                    copy.start()
                    later.append(copy)

    for c in range(len(chunks)):
        for way in range(2):
            send_step(way, 0, c)
        if c == (len(chunks) - 1) // 2:
            issue(0)
    issue(1)

    for hop, needed, start in plan:
        @pl.when(tm < hop)
        def _():
            counts[hop] = jnp.zeros(counts.shape[1:], jnp.int32)
            kv_win[:, start:start + needed] = jnp.zeros(
                (2, needed) + kv_win.shape[2:], kv_win.dtype)

    for hop, copy in count_copies:
        pl.when(tm >= hop)(copy.wait_recv)
    own_copies[0].wait()
    own_copies[1].wait()

    slots = tile * tokens + lax.broadcasted_iota(jnp.int32, (tokens, LANES), 0)
    first_lane = lax.broadcasted_iota(jnp.int32, (tokens, LANES), 1) == 0
    for w in range(LEAD + frames):
        if w >= LEAD:
            row = counts[0, w - LEAD:w - LEAD + 1, :]
        else:
            hop, needed, start = [p for p in plan if p[2] <= w < p[2] + p[1]][0]
            at = frames - needed + w - start
            row = counts[hop, at:at + 1, :]
        bias[w] = jnp.where(
            jnp.logical_and(first_lane, slots >= row), DEAD, 0.0).astype(bias.dtype)

    keys = WINDOW * tokens
    unit_lane = (
        lax.broadcasted_iota(jnp.int32, (groups * tokens, LANES), 1) == 0
    ).astype(jnp.bfloat16)
    ones = jnp.ones((keys, LANES), jnp.bfloat16)
    scale = HEAD_DIM ** (-0.5) * LOG2E
    exchanged = []
    taken = 0
    relay(0)
    for unit in range(KVHEADS * frames):
        g, f = unit // frames, unit % frames
        if f == 0:
            if taken < steps - 1:
                take(taken, 0)
            issue(g + 2)
            arrive(g)
        if f == frames - 1:
            if taken < steps - 1:
                take(taken, 1)
                taken += 1
            if g + 1 < KVHEADS:
                relay(g + 1)
        span = slice(g * HEAD_DIM, (g + 1) * HEAD_DIM)
        k = kv_win[0, f:f + WINDOW, :, span].reshape(keys, HEAD_DIM)
        v = kv_win[1, f:f + WINDOW, :, span].reshape(keys, HEAD_DIM)
        k = jnp.concatenate([k, bias[f:f + WINDOW].reshape(keys, LANES)], axis=1)
        v = jnp.concatenate([v, ones], axis=1)
        q = jnp.concatenate(
            [q_buf[f, :, (g * groups + i) * HEAD_DIM:(g * groups + i + 1) * HEAD_DIM]
             for i in range(groups)], axis=0)
        q = jnp.concatenate([q, unit_lane], axis=1)
        scores = lax.dot_general(q, k, (((1,), (1,)), ((), ())), preferred_element_type=jnp.float32)
        top = jnp.max(scores, axis=-1, keepdims=True)
        weights = jnp.exp2((scores - top) * scale).astype(jnp.bfloat16)
        mixed = jnp.dot(weights, v, preferred_element_type=jnp.float32)
        result = (mixed[:, :HEAD_DIM] / mixed[:, HEAD_DIM:]).astype(jnp.bfloat16)
        for i in range(groups):
            at = (g * groups + i) * HEAD_DIM
            att[f, tile, :, at:at + HEAD_DIM] = result[i * tokens:(i + 1) * tokens]
        if tiles == 2:
            part = att.at[f, tile, :, g * groups * HEAD_DIM:(g + 1) * groups * HEAD_DIM]
            copy = pltpu.make_async_remote_copy(
                src_ref=part, dst_ref=part,
                send_sem=tile_send.at[unit], recv_sem=tile_recv.at[unit],
                device_id={"tile": 1 - tile}, device_id_type=MESH)
            copy.start()
            exchanged.append(copy)
    while taken < steps:
        before_last = list(later)
        take(taken, 0)
        take(taken, 1)
        taken += 1

    columns = w_ref.shape[1]
    same = (
        lax.rem(lax.broadcasted_iota(jnp.int32, (2 * LANES, LANES), 0), LANES) // IDM_DIM
        == lax.broadcasted_iota(jnp.int32, (2 * LANES, LANES), 1) // IDM_DIM
    ).astype(jnp.bfloat16)
    own_copies[2].wait()
    for copy in exchanged:
        copy.wait_recv()

    def projected(f, owners):
        if owners is None:
            return jnp.dot(
                att[f].reshape(tiles * tokens, width), w_full[...].reshape(n * rows, columns),
                preferred_element_type=jnp.float32)
        parts = []
        for owner in owners:
            span = pl.ds(pl.multiple_of(owner * rows, LANES), rows)
            parts.append(jnp.dot(
                att[f, :, :, span].reshape(tiles * tokens, rows), w_full[owner],
                preferred_element_type=jnp.float32))
        return sum(parts)

    first_wave, last_wave = [tm], None
    by_clip = before_last if steps else []
    if rows % LANES == 0 and steps > 1:
        for step in range(steps - 1):
            first_wave += [index_of(place - step - 1), index_of(place + step + 1)]
        last_wave = [index_of(place - steps)]
        if n % 2:
            last_wave.append(index_of(place + steps))
        for copy in by_clip:
            copy.wait_recv()
        for f in range(frames):
            total_ref[f] = projected(f, first_wave)
    else:
        by_clip = []
    for copy in later[len(by_clip):]:
        copy.wait_recv()
    for f in range(frames):
        latent = projected(f, last_wave)
        if last_wave is not None:
            latent = latent + total_ref[f]
        latent = latent.astype(jnp.bfloat16).astype(jnp.float32)
        for c in range(0, columns, LANES):
            value = latent[:, c:c + LANES]
            square = value * value
            high = square.astype(jnp.bfloat16)
            low = (square - high.astype(jnp.float32)).astype(jnp.bfloat16)
            total = jnp.dot(
                jnp.concatenate([high, low], axis=1), same, preferred_element_type=jnp.float32)
            scaled = value * lax.rsqrt(total * (1.0 / IDM_DIM) + 1e-6) * gain_ref[:, c:c + LANES]
            out_ref[f, :, c:c + LANES] = scaled.astype(out_ref.dtype)

    for copy in started + later + exchanged:
        copy.wait_send()
    for hop, copy in count_copies:
        pl.when(tm + hop < n)(copy.wait_send)
    for group in firsts + relays:
        for entry in group:
            pl.when(entry[1])(entry[0].wait_send)


def normed_latent(mesh, queries, keyvals, proj_weight, norm_gain, frame_counts):
    n, clips, tiles = (mesh.shape[a] for a in ("tm", "clip", "tile"))
    frames, tokens, width = queries.shape
    rows, columns = proj_weight.shape
    plan = halo_plan(frames)
    hops = len(plan)
    rest = max(1, plan[0][1] - plan[1][1]) if hops > 1 else 1
    roles = max(8, hops) * KVHEADS
    steps = max(1, n // 2)
    units = frames * KVHEADS
    dma = pltpu.SemaphoreType.DMA
    hbm = pl.BlockSpec(memory_space=pltpu.HBM)
    vmem = pl.BlockSpec(memory_space=pltpu.VMEM)
    bf16 = jnp.bfloat16
    flops = frames * tokens * width * 4 * WINDOW * tokens + 2 * frames * tiles * tokens * width * columns
    return pl.pallas_call(
        functools.partial(latent_kernel, n, clips, tiles, columns_of(mesh)),
        out_shape=jax.ShapeDtypeStruct((frames, tiles * tokens, columns), bf16),
        in_specs=[pl.BlockSpec(memory_space=pltpu.SMEM), hbm, hbm, hbm, vmem],
        out_specs=vmem,
        scratch_shapes=[
            pltpu.VMEM(queries.shape, bf16),
            pltpu.VMEM((2, LEAD + frames) + keyvals.shape[2:], bf16),
            pltpu.VMEM((1, rest) + keyvals.shape[2:], bf16),
            pltpu.VMEM((n, rows, columns), bf16),
            pltpu.VMEM((frames, tiles, tokens, width), bf16),
            pltpu.VMEM((frames, tiles * tokens, columns), jnp.float32),
            pltpu.VMEM((hops + 1, max(8, frames), LANES), jnp.int32),
            pltpu.VMEM((LEAD + frames, tokens, LANES), bf16),
            dma((3,)), dma((roles,)), dma((roles,)), dma((hops,)), dma((hops,)),
            dma((8 * steps,)), dma((8 * steps,)), dma((8 * steps,)), dma((8 * steps,)),
            dma((units,)), dma((units,)),
        ],
        compiler_params=pltpu.CompilerParams(
            collective_id=0, has_side_effects=True, vmem_limit_bytes=60 * 2 ** 20),
        cost_estimate=pl.CostEstimate(
            flops=flops, bytes_accessed=8 * 2 ** 20, transcendentals=0),
    )(frame_counts, queries, keyvals, proj_weight, norm_gain.reshape(1, -1))


def partner_kernel(sources, counts_ref, *refs):
    out_ref = refs[-1]
    frame = pl.program_id(0)
    tokens, columns = out_ref.shape[1:]
    keys = sources * tokens
    slots = lax.broadcasted_iota(jnp.int32, (tokens, LANES), 0)
    live = jnp.concatenate(
        [slots < counts_ref[source, frame] for source in range(sources)], axis=0)
    lower = lax.broadcasted_iota(jnp.int32, (tokens, LANES), 1) < IDM_DIM
    scale = IDM_DIM ** (-0.5) * LOG2E
    for c in range(0, columns, LANES):
        k = jnp.concatenate([ref[0, :, c:c + LANES] for ref in refs[:sources]], axis=0)
        q = refs[0][0, :, c:c + LANES]
        zero = jnp.zeros_like(q)
        q = jnp.concatenate([jnp.where(lower, q, zero), jnp.where(lower, zero, q)], axis=0)
        v = jnp.concatenate(
            [jnp.where(live, k, jnp.zeros_like(k)), live.astype(k.dtype)], axis=1)
        scores = lax.dot_general(q, k, (((1,), (1,)), ((), ())), preferred_element_type=jnp.float32)
        weights = jnp.exp2(scores * scale).astype(jnp.bfloat16)
        mixed = jnp.dot(weights, v, preferred_element_type=jnp.float32)
        total = jnp.where(lower, mixed[:tokens, LANES:], mixed[tokens:, LANES:])
        result = jnp.where(lower, mixed[:tokens, :LANES], mixed[tokens:, :LANES]) / total
        out_ref[0, :, c:c + LANES] = result.astype(out_ref.dtype)


def partner_attention(counts, blocks):
    frames, tokens, columns = blocks[0].shape
    spec = pl.BlockSpec((1, tokens, columns), lambda f: (f, 0, 0))
    return pl.pallas_call(
        functools.partial(partner_kernel, len(blocks)),
        out_shape=jax.ShapeDtypeStruct(blocks[0].shape, jnp.bfloat16),
        grid=(frames,),
        in_specs=[pl.BlockSpec(memory_space=pltpu.SMEM)] + [spec] * len(blocks),
        out_specs=spec,
        compiler_params=pltpu.CompilerParams(vmem_limit_bytes=60 * 2 ** 20),
    )(counts, *blocks)


def local(mesh, queries, keyvals, proj_weight, norm_gain, frame_counts):
    normed = normed_latent(mesh, queries, keyvals, proj_weight, norm_gain, frame_counts)
    distance = PARTNER // queries.shape[0]
    blocks, counts = [normed], [frame_counts]
    for steps in (distance, -distance):
        if distance < mesh.shape["tm"]:
            block, count = passed_along((normed, frame_counts), "tm", steps)
            blocks.append(block)
            counts.append(count)
    return partner_attention(jnp.stack(counts), blocks)


def solution(mesh):
    in_specs = (
        P(("clip", "tm"), "tile", None),
        P(None, ("clip", "tm"), "tile", None),
        P("tm", "tile"),
        P("tile"),
        P(("clip", "tm")),
    )
    out_specs = P(("clip", "tm"), None, "tile")
    return jax.shard_map(
        functools.partial(local, mesh), mesh=mesh, in_specs=in_specs, out_specs=out_specs,
        check_vma=False)
```

```python
import functools
import math

import jax
import jax.numpy as jnp
from jax import lax
from jax.experimental import pallas as pl
from jax.experimental.pallas import tpu as pltpu
from jax.sharding import PartitionSpec as P

QHEADS = 16
KVHEADS = 4
HEAD_DIM = 128
IDM_DIM = 64
WINDOW = 4
PARTNER = 16
LEAD = WINDOW - 1
LANES = 128
TILE_ROWS = 16
DEAD = -1e30
LOG2E = math.log2(math.e)
MESH = pl.DeviceIdType.MESH


def passed_along(value, axis, steps):
    count = lax.axis_size(axis)
    initial, last = (max(0, -steps), min(count, count - steps))
    return lax.ppermute(value, axis, [(source, source + steps) for source in range(initial, last)])


def columns_of(mesh):
    place = mesh.axis_names.index("tm")
    line = mesh.devices.transpose(
        [place] + [i for i in range(mesh.devices.ndim) if i != place]
    ).reshape(mesh.shape["tm"], -1)[:, 0]
    coords = [getattr(device, "coords", None) for device in line]
    if coords[0] is None or len(line) == 1:
        return 1
    moved = [i for i in range(len(coords[0])) if coords[0][i] != coords[1][i]]
    if len(moved) != 1:
        return 1
    columns = len({c[moved[0]] for c in coords})
    return columns if len(line) % columns == 0 else 1


def halo_plan(frames):
    plan, covered, hop = [], 0, 1
    while covered < LEAD:
        needed = min(frames, LEAD - covered)
        covered += needed
        plan.append((hop, needed, LEAD - covered))
        hop += 1
    return plan


def relayed(plan, x_count, n):
    return x_count == 2 and n % 2 == 0 and len(plan) == 2 and plan[0][1] > plan[1][1]


def ring_chunks(rows, clip, clips):
    over = clips == 2 and rows % (2 * TILE_ROWS) == 0
    start, size = (clip * (rows // 2), rows // 2) if over else (0, rows)
    if size % (2 * TILE_ROWS):
        return [(start, size, over)]
    return [(start, size // 2, over), (start + size // 2, size // 2, over)]


def latent_kernel(
    n, clips, tiles, x_count,
    counts_ref, q_ref, kv_ref, w_ref, gain_ref, out_ref,
    q_buf, kv_win, stash, w_full, att, total_ref, counts, bias,
    local_sem, halo_send, halo_recv, count_send, count_recv,
    ring_send, ring_recv, clip_send, clip_recv, tile_send, tile_recv,
):
    clip, tm, tile = lax.axis_index("clip"), lax.axis_index("tm"), lax.axis_index("tile")
    frames, tokens, width = q_ref.shape
    rows = w_ref.shape[0]
    groups = QHEADS // KVHEADS
    plan = halo_plan(frames)
    z_count = n // x_count

    def place_of(index):
        x, z = lax.rem(index, x_count), index // x_count
        return x * z_count + z + lax.rem(x, 2) * (z_count - 1 - 2 * z)

    def index_of(place):
        place = lax.rem(place + 2 * n, n)
        x, z = place // z_count, lax.rem(place, z_count)
        return (z + lax.rem(x, 2) * (z_count - 1 - 2 * z)) * x_count + x

    place = place_of(tm)
    ends = (index_of(place + 1), index_of(place - 1))

    own_copies = [
        pltpu.make_async_copy(kv_ref, kv_win.at[:, LEAD:LEAD + frames], local_sem.at[0]),
        pltpu.make_async_copy(q_ref, q_buf, local_sem.at[1]),
        pltpu.make_async_copy(w_ref, w_full.at[tm], local_sem.at[2]),
    ]
    for copy in own_copies:
        copy.start()

    barrier = pltpu.get_barrier_semaphore()
    expected = 0
    if n > 1:
        for end in ends:
            pl.semaphore_signal(barrier, inc=1, device_id={"tm": end}, device_id_type=MESH)
            expected += 1
    if clips == 2:
        pl.semaphore_signal(barrier, inc=1, device_id={"clip": 1 - clip}, device_id_type=MESH)
        expected += 1
    if tiles == 2:
        pl.semaphore_signal(barrier, inc=1, device_id={"tile": 1 - tile}, device_id_type=MESH)
        expected += 1
    for hop, _, _ in plan:
        @pl.when(tm + hop < n)
        def _():
            pl.semaphore_signal(barrier, inc=1, device_id={"tm": tm + hop}, device_id_type=MESH)

        @pl.when(tm >= hop)
        def _():
            pl.semaphore_signal(barrier, inc=1, device_id={"tm": tm - hop}, device_id_type=MESH)

        expected = expected + jnp.where(tm + hop < n, 1, 0) + jnp.where(tm >= hop, 1, 0)
    for f in range(frames):
        counts[0, f:f + 1, :] = jnp.full((1, LANES), counts_ref[f], jnp.int32)
    pl.semaphore_wait(barrier, expected)

    count_copies = []
    for i, (hop, _, _) in enumerate(plan):
        count_copies.append((hop, pltpu.make_async_remote_copy(
            src_ref=counts.at[0], dst_ref=counts.at[hop],
            send_sem=count_send.at[i], recv_sem=count_recv.at[i],
            device_id={"tm": lax.rem(tm + hop, n)}, device_id_type=MESH)))
    for hop, copy in count_copies:
        pl.when(tm + hop < n)(copy.start)

    def halo_copy(role, arrival, g, source, first, count, place_at, hop):
        span = pl.ds(g * HEAD_DIM, HEAD_DIM)
        target = stash if place_at is None else kv_win.at[:, place_at:place_at + count]
        return pltpu.make_async_remote_copy(
            src_ref=source.at[:, first:first + count, :, span],
            dst_ref=target.at[:, :, :, span],
            send_sem=halo_send.at[role * KVHEADS + g],
            recv_sem=halo_recv.at[arrival * KVHEADS + g],
            device_id={"tm": lax.rem(tm + hop + n, n)}, device_id_type=MESH)

    firsts, relays, arrivals = [[] for _ in range(KVHEADS)], [], []
    if relayed(plan, x_count, n):
        (_, needed, start), (_, last, start2) = plan
        rest = needed - last
        even, odd = lax.rem(tm, 2) == 0, lax.rem(tm, 2) == 1
        up, down = tm + 2 < n, tm >= 2
        for g in range(KVHEADS):
            firsts[g] += [
                (halo_copy(2, 2, g, kv_ref, frames - last, last, start2, 2), up),
                (halo_copy(3, 3, g, kv_ref, frames - needed, rest, None, -1),
                 jnp.logical_and(odd, up)),
                (halo_copy(0, 0, g, kv_ref, frames - needed, rest, start, 1), even),
                (halo_copy(1, 1, g, kv_ref, frames - last, last, start + rest, 1), even),
            ]
            relays.append([
                (halo_copy(4, 0, g, stash, 0, rest, start, 2), jnp.logical_and(even, up), 3),
                (halo_copy(5, 1, g, kv_win, start2, last, start + rest, -1),
                 jnp.logical_and(odd, down), 2),
            ])
            arrivals.append([
                (0, tm >= 1, rest, start), (1, tm >= 1, last, start + rest),
                (2, jnp.logical_and(even, down), last, start2),
            ])
    else:
        for g in range(KVHEADS):
            for i, (hop, needed, start) in enumerate(plan):
                firsts[g].append((
                    halo_copy(i, i, g, kv_ref, frames - needed, needed, start, hop), tm + hop < n))
            relays.append([])
            arrivals.append([
                (i, tm >= hop, needed, start) for i, (hop, needed, start) in enumerate(plan)])

    def issue(g):
        if g < KVHEADS:
            for copy, mine in firsts[g]:
                pl.when(mine)(copy.start)

    def arrival_of(arrival, g, count, place_at):
        return halo_copy(0, arrival, g, kv_ref, 0, count, place_at, 1)

    def relay(g):
        for copy, mine, arrival in relays[g]:
            @pl.when(mine)
            def _():
                count, place_at = (rest, None) if arrival == 3 else (last, start2)
                arrival_of(arrival, g, count, place_at).wait_recv()
                copy.start()

    def arrive(g):
        for arrival, mine, count, place_at in arrivals[g]:
            pl.when(mine)(arrival_of(arrival, g, count, place_at).wait_recv)

    chunks = ring_chunks(rows, clip, clips)
    steps = n // 2
    started, later = [], []

    def ring_copy(way, step, c):
        start, size, _ = chunks[c]
        owner = index_of(place - step * (1 - 2 * way))
        span = pl.ds(start if isinstance(start, int) else pl.multiple_of(start, TILE_ROWS), size)
        slot = (way * max(steps, 1) + step) * len(chunks) + c
        return pltpu.make_async_remote_copy(
            src_ref=w_ref.at[span] if step == 0 else w_full.at[owner, span],
            dst_ref=w_full.at[owner, span],
            send_sem=ring_send.at[slot], recv_sem=ring_recv.at[slot],
            device_id={"tm": ends[way]}, device_id_type=MESH)

    def goes(way, step, c):
        return n % 2 == 1 or step < steps - 1 or c % 2 == way

    def send_step(way, step, c):
        if step < steps and goes(way, step, c):
            copy = ring_copy(way, step, c)
            copy.start()
            started.append(copy)

    def take(step, c):
        if c < len(chunks):
            for way in range(2):
                if not goes(way, step, c):
                    continue
                ring_copy(way, step, c).wait_recv()
                send_step(way, step + 1, c)
                start, size, over = chunks[c]
                if over:
                    owner = index_of(place - (step + 1) * (1 - 2 * way))
                    span = pl.ds(pl.multiple_of(start, TILE_ROWS), size)
                    slot = (way * steps + step) * len(chunks) + c
                    copy = pltpu.make_async_remote_copy(
                        src_ref=w_full.at[owner, span], dst_ref=w_full.at[owner, span],
                        send_sem=clip_send.at[slot], recv_sem=clip_recv.at[slot],
                        device_id={"clip": 1 - clip}, device_id_type=MESH)
                    copy.start()
                    later.append(copy)

    for c in range(len(chunks)):
        issue(c)
        for way in range(2):
            send_step(way, 0, c)
    for g in range(len(chunks), 3):
        issue(g)

    for hop, needed, start in plan:
        @pl.when(tm < hop)
        def _():
            counts[hop] = jnp.zeros(counts.shape[1:], jnp.int32)
            kv_win[:, start:start + needed] = jnp.zeros(
                (2, needed) + kv_win.shape[2:], kv_win.dtype)

    for hop, copy in count_copies:
        pl.when(tm >= hop)(copy.wait_recv)
    own_copies[0].wait()
    own_copies[1].wait()

    slots = tile * tokens + lax.broadcasted_iota(jnp.int32, (tokens, LANES), 0)
    first_lane = lax.broadcasted_iota(jnp.int32, (tokens, LANES), 1) == 0
    for w in range(LEAD + frames):
        if w >= LEAD:
            row = counts[0, w - LEAD:w - LEAD + 1, :]
        else:
            hop, needed, start = [p for p in plan if p[2] <= w < p[2] + p[1]][0]
            at = frames - needed + w - start
            row = counts[hop, at:at + 1, :]
        bias[w] = jnp.where(
            jnp.logical_and(first_lane, slots >= row), DEAD, 0.0).astype(bias.dtype)

    keys = WINDOW * tokens
    unit_lane = (
        lax.broadcasted_iota(jnp.int32, (groups * tokens, LANES), 1) == 0
    ).astype(jnp.bfloat16)
    ones = jnp.ones((keys, LANES), jnp.bfloat16)
    scale = HEAD_DIM ** (-0.5) * LOG2E
    exchanged = []
    taken = 0
    relay(0)
    for unit in range(KVHEADS * frames):
        g, f = unit // frames, unit % frames
        if f == 0:
            if taken < steps - 1:
                take(taken, 0)
            issue(g + 3)
            arrive(g)
        if f == frames - 1:
            if g + 1 < KVHEADS:
                relay(g + 1)
            if taken < steps - 1:
                take(taken, 1)
                taken += 1
        span = slice(g * HEAD_DIM, (g + 1) * HEAD_DIM)
        k = kv_win[0, f:f + WINDOW, :, span].reshape(keys, HEAD_DIM)
        v = kv_win[1, f:f + WINDOW, :, span].reshape(keys, HEAD_DIM)
        k = jnp.concatenate([k, bias[f:f + WINDOW].reshape(keys, LANES)], axis=1)
        v = jnp.concatenate([v, ones], axis=1)
        q = jnp.concatenate(
            [q_buf[f, :, (g * groups + i) * HEAD_DIM:(g * groups + i + 1) * HEAD_DIM]
             for i in range(groups)], axis=0)
        q = jnp.concatenate([q, unit_lane], axis=1)
        scores = lax.dot_general(q, k, (((1,), (1,)), ((), ())), preferred_element_type=jnp.float32)
        top = jnp.max(scores, axis=-1, keepdims=True)
        weights = jnp.exp2((scores - top) * scale).astype(jnp.bfloat16)
        mixed = jnp.dot(weights, v, preferred_element_type=jnp.float32)
        result = (mixed[:, :HEAD_DIM] / mixed[:, HEAD_DIM:]).astype(jnp.bfloat16)
        for i in range(groups):
            at = (g * groups + i) * HEAD_DIM
            att[f, tile, :, at:at + HEAD_DIM] = result[i * tokens:(i + 1) * tokens]
        if tiles == 2:
            part = att.at[f, tile, :, g * groups * HEAD_DIM:(g + 1) * groups * HEAD_DIM]
            copy = pltpu.make_async_remote_copy(
                src_ref=part, dst_ref=part,
                send_sem=tile_send.at[unit], recv_sem=tile_recv.at[unit],
                device_id={"tile": 1 - tile}, device_id_type=MESH)
            copy.start()
            exchanged.append(copy)
    while taken < steps:
        before_last = list(later)
        take(taken, 0)
        take(taken, 1)
        taken += 1

    columns = w_ref.shape[1]
    same = (
        lax.rem(lax.broadcasted_iota(jnp.int32, (2 * LANES, LANES), 0), LANES) // IDM_DIM
        == lax.broadcasted_iota(jnp.int32, (2 * LANES, LANES), 1) // IDM_DIM
    ).astype(jnp.bfloat16)
    own_copies[2].wait()
    for copy in exchanged:
        copy.wait_recv()

    def projected(f, owners):
        if owners is None:
            return jnp.dot(
                att[f].reshape(tiles * tokens, width), w_full[...].reshape(n * rows, columns),
                preferred_element_type=jnp.float32)
        parts = []
        for owner in owners:
            span = pl.ds(pl.multiple_of(owner * rows, LANES), rows)
            parts.append(jnp.dot(
                att[f, :, :, span].reshape(tiles * tokens, rows), w_full[owner],
                preferred_element_type=jnp.float32))
        return sum(parts)

    first_wave, last_wave = [tm], None
    by_clip = before_last if steps else []
    if rows % LANES == 0 and steps > 1:
        for step in range(steps - 1):
            first_wave += [index_of(place - step - 1), index_of(place + step + 1)]
        last_wave = [index_of(place - steps)]
        if n % 2:
            last_wave.append(index_of(place + steps))
        for copy in by_clip:
            copy.wait_recv()
        for f in range(frames):
            total_ref[f] = projected(f, first_wave)
    else:
        by_clip = []
    for copy in later[len(by_clip):]:
        copy.wait_recv()
    for f in range(frames):
        latent = projected(f, last_wave)
        if last_wave is not None:
            latent = latent + total_ref[f]
        latent = latent.astype(jnp.bfloat16).astype(jnp.float32)
        for c in range(0, columns, LANES):
            value = latent[:, c:c + LANES]
            square = value * value
            high = square.astype(jnp.bfloat16)
            low = (square - high.astype(jnp.float32)).astype(jnp.bfloat16)
            total = jnp.dot(
                jnp.concatenate([high, low], axis=1), same, preferred_element_type=jnp.float32)
            scaled = value * lax.rsqrt(total * (1.0 / IDM_DIM) + 1e-6) * gain_ref[:, c:c + LANES]
            out_ref[f, :, c:c + LANES] = scaled.astype(out_ref.dtype)

    for copy in started + later + exchanged:
        copy.wait_send()
    for hop, copy in count_copies:
        pl.when(tm + hop < n)(copy.wait_send)
    for group in firsts + relays:
        for entry in group:
            pl.when(entry[1])(entry[0].wait_send)


def normed_latent(mesh, queries, keyvals, proj_weight, norm_gain, frame_counts):
    n, clips, tiles = (mesh.shape[a] for a in ("tm", "clip", "tile"))
    frames, tokens, width = queries.shape
    rows, columns = proj_weight.shape
    plan = halo_plan(frames)
    hops = len(plan)
    rest = max(1, plan[0][1] - plan[1][1]) if hops > 1 else 1
    roles = max(6, hops) * KVHEADS
    steps = max(1, n // 2)
    units = frames * KVHEADS
    dma = pltpu.SemaphoreType.DMA
    hbm = pl.BlockSpec(memory_space=pltpu.HBM)
    vmem = pl.BlockSpec(memory_space=pltpu.VMEM)
    bf16 = jnp.bfloat16
    flops = frames * tokens * width * 4 * WINDOW * tokens + 2 * frames * tiles * tokens * width * columns
    return pl.pallas_call(
        functools.partial(latent_kernel, n, clips, tiles, columns_of(mesh)),
        out_shape=jax.ShapeDtypeStruct((frames, tiles * tokens, columns), bf16),
        in_specs=[pl.BlockSpec(memory_space=pltpu.SMEM), hbm, hbm, hbm, vmem],
        out_specs=vmem,
        scratch_shapes=[
            pltpu.VMEM(queries.shape, bf16),
            pltpu.VMEM((2, LEAD + frames) + keyvals.shape[2:], bf16),
            pltpu.VMEM((2, rest) + keyvals.shape[2:], bf16),
            pltpu.VMEM((n, rows, columns), bf16),
            pltpu.VMEM((frames, tiles, tokens, width), bf16),
            pltpu.VMEM((frames, tiles * tokens, columns), jnp.float32),
            pltpu.VMEM((hops + 1, max(8, frames), LANES), jnp.int32),
            pltpu.VMEM((LEAD + frames, tokens, LANES), bf16),
            dma((3,)), dma((roles,)), dma((roles,)), dma((hops,)), dma((hops,)),
            dma((4 * steps,)), dma((4 * steps,)), dma((4 * steps,)), dma((4 * steps,)),
            dma((units,)), dma((units,)),
        ],
        compiler_params=pltpu.CompilerParams(
            collective_id=0, has_side_effects=True, vmem_limit_bytes=60 * 2 ** 20),
        cost_estimate=pl.CostEstimate(
            flops=flops, bytes_accessed=8 * 2 ** 20, transcendentals=0),
    )(frame_counts, queries, keyvals, proj_weight, norm_gain.reshape(1, -1))


def partner_kernel(sources, counts_ref, *refs):
    out_ref = refs[-1]
    frame = pl.program_id(0)
    tokens, columns = out_ref.shape[1:]
    keys = sources * tokens
    slots = lax.broadcasted_iota(jnp.int32, (tokens, LANES), 0)
    live = jnp.concatenate(
        [slots < counts_ref[source, frame] for source in range(sources)], axis=0)
    lower = lax.broadcasted_iota(jnp.int32, (tokens, LANES), 1) < IDM_DIM
    scale = IDM_DIM ** (-0.5) * LOG2E
    for c in range(0, columns, LANES):
        k = jnp.concatenate([ref[0, :, c:c + LANES] for ref in refs[:sources]], axis=0)
        q = refs[0][0, :, c:c + LANES]
        zero = jnp.zeros_like(q)
        q = jnp.concatenate([jnp.where(lower, q, zero), jnp.where(lower, zero, q)], axis=0)
        v = jnp.concatenate(
            [jnp.where(live, k, jnp.zeros_like(k)), live.astype(k.dtype)], axis=1)
        scores = lax.dot_general(q, k, (((1,), (1,)), ((), ())), preferred_element_type=jnp.float32)
        weights = jnp.exp2(scores * scale).astype(jnp.bfloat16)
        mixed = jnp.dot(weights, v, preferred_element_type=jnp.float32)
        result = mixed[:, :LANES] / mixed[:, LANES:]
        out_ref[0, :, c:c + LANES] = jnp.where(
            lower, result[:tokens], result[tokens:]).astype(out_ref.dtype)


def partner_attention(counts, blocks):
    frames, tokens, columns = blocks[0].shape
    part = 2 * LANES if columns % (2 * LANES) == 0 else columns
    spec = pl.BlockSpec((1, tokens, part), lambda f, c: (f, 0, c))
    return pl.pallas_call(
        functools.partial(partner_kernel, len(blocks)),
        out_shape=jax.ShapeDtypeStruct(blocks[0].shape, jnp.bfloat16),
        grid=(frames, columns // part),
        in_specs=[pl.BlockSpec(memory_space=pltpu.SMEM)] + [spec] * len(blocks),
        out_specs=spec,
        compiler_params=pltpu.CompilerParams(vmem_limit_bytes=60 * 2 ** 20),
    )(counts, *blocks)


def local(mesh, queries, keyvals, proj_weight, norm_gain, frame_counts):
    normed = normed_latent(mesh, queries, keyvals, proj_weight, norm_gain, frame_counts)
    distance = PARTNER // queries.shape[0]
    blocks, counts = [normed], [frame_counts]
    for steps in (distance, -distance):
        if distance < mesh.shape["tm"]:
            block, count = passed_along((normed, frame_counts), "tm", steps)
            blocks.append(block)
            counts.append(count)
    return partner_attention(jnp.stack(counts), blocks)


def solution(mesh):
    in_specs = (
        P(("clip", "tm"), "tile", None),
        P(None, ("clip", "tm"), "tile", None),
        P("tm", "tile"),
        P("tile"),
        P(("clip", "tm")),
    )
    out_specs = P(("clip", "tm"), None, "tile")
    return jax.shard_map(
        functools.partial(local, mesh), mesh=mesh, in_specs=in_specs, out_specs=out_specs,
        check_vma=False)
```

```python
import functools
import math

import jax
import jax.numpy as jnp
from jax import lax
from jax.experimental import pallas as pl
from jax.experimental.pallas import tpu as pltpu
from jax.sharding import PartitionSpec as P

QHEADS = 16
KVHEADS = 4
HEAD_DIM = 128
IDM_DIM = 64
WINDOW = 4
PARTNER = 16
LEAD = WINDOW - 1
LANES = 128
TILE_ROWS = 16
DEAD = -1e30
LOG2E = math.log2(math.e)
MESH = pl.DeviceIdType.MESH


def passed_along(value, axis, steps):
    count = lax.axis_size(axis)
    initial, last = (max(0, -steps), min(count, count - steps))
    return lax.ppermute(value, axis, [(source, source + steps) for source in range(initial, last)])


def columns_of(mesh):
    place = mesh.axis_names.index("tm")
    line = mesh.devices.transpose(
        [place] + [i for i in range(mesh.devices.ndim) if i != place]
    ).reshape(mesh.shape["tm"], -1)[:, 0]
    coords = [getattr(device, "coords", None) for device in line]
    if coords[0] is None or len(line) == 1:
        return 1
    moved = [i for i in range(len(coords[0])) if coords[0][i] != coords[1][i]]
    if len(moved) != 1:
        return 1
    columns = len({c[moved[0]] for c in coords})
    return columns if len(line) % columns == 0 else 1


def halo_plan(frames):
    plan, covered, hop = [], 0, 1
    while covered < LEAD:
        needed = min(frames, LEAD - covered)
        covered += needed
        plan.append((hop, needed, LEAD - covered))
        hop += 1
    return plan


def relayed(plan, x_count, n):
    return x_count == 2 and n % 2 == 0 and len(plan) == 2 and plan[0][1] > plan[1][1]


def ring_chunks(rows, clip, clips):
    over = clips == 2 and rows % (2 * TILE_ROWS) == 0
    start, size = (clip * (rows // 2), rows // 2) if over else (0, rows)
    if size % (2 * TILE_ROWS):
        return [(start, size, over)]
    return [(start, size // 2, over), (start + size // 2, size // 2, over)]


def latent_kernel(
    n, clips, tiles, x_count,
    counts_ref, q_ref, kv_ref, w_ref, gain_ref, out_ref,
    q_buf, kv_win, stash, w_full, att, total_ref, counts, bias,
    local_sem, halo_send, halo_recv, count_send, count_recv,
    ring_send, ring_recv, clip_send, clip_recv, tile_send, tile_recv,
):
    clip, tm, tile = lax.axis_index("clip"), lax.axis_index("tm"), lax.axis_index("tile")
    frames, tokens, width = q_ref.shape
    rows = w_ref.shape[0]
    groups = QHEADS // KVHEADS
    plan = halo_plan(frames)
    z_count = n // x_count

    def place_of(index):
        x, z = lax.rem(index, x_count), index // x_count
        return x * z_count + z + lax.rem(x, 2) * (z_count - 1 - 2 * z)

    def index_of(place):
        place = lax.rem(place + 2 * n, n)
        x, z = place // z_count, lax.rem(place, z_count)
        return (z + lax.rem(x, 2) * (z_count - 1 - 2 * z)) * x_count + x

    place = place_of(tm)
    ends = (index_of(place + 1), index_of(place - 1))

    own_copies = [
        pltpu.make_async_copy(kv_ref, kv_win.at[:, LEAD:LEAD + frames], local_sem.at[0]),
        pltpu.make_async_copy(q_ref, q_buf, local_sem.at[1]),
        pltpu.make_async_copy(w_ref, w_full.at[tm], local_sem.at[2]),
    ]
    for copy in own_copies:
        copy.start()

    barrier = pltpu.get_barrier_semaphore()
    expected = 0
    if n > 1:
        for end in ends:
            pl.semaphore_signal(barrier, inc=1, device_id={"tm": end}, device_id_type=MESH)
            expected += 1
    if clips == 2:
        pl.semaphore_signal(barrier, inc=1, device_id={"clip": 1 - clip}, device_id_type=MESH)
        expected += 1
    if tiles == 2:
        pl.semaphore_signal(barrier, inc=1, device_id={"tile": 1 - tile}, device_id_type=MESH)
        expected += 1
    for hop, _, _ in plan:
        @pl.when(tm + hop < n)
        def _():
            pl.semaphore_signal(barrier, inc=1, device_id={"tm": tm + hop}, device_id_type=MESH)

        @pl.when(tm >= hop)
        def _():
            pl.semaphore_signal(barrier, inc=1, device_id={"tm": tm - hop}, device_id_type=MESH)

        expected = expected + jnp.where(tm + hop < n, 1, 0) + jnp.where(tm >= hop, 1, 0)
    for f in range(frames):
        counts[0, f:f + 1, :] = jnp.full((1, LANES), counts_ref[f], jnp.int32)
    pl.semaphore_wait(barrier, expected)

    count_copies = []
    for i, (hop, _, _) in enumerate(plan):
        count_copies.append((hop, pltpu.make_async_remote_copy(
            src_ref=counts.at[0], dst_ref=counts.at[hop],
            send_sem=count_send.at[i], recv_sem=count_recv.at[i],
            device_id={"tm": lax.rem(tm + hop, n)}, device_id_type=MESH)))
    for hop, copy in count_copies:
        pl.when(tm + hop < n)(copy.start)

    def halo_copy(role, arrival, g, source, first, count, place_at, hop):
        span = pl.ds(g * HEAD_DIM, HEAD_DIM)
        target = stash if place_at is None else kv_win.at[:, place_at:place_at + count]
        return pltpu.make_async_remote_copy(
            src_ref=source.at[:, first:first + count, :, span],
            dst_ref=target.at[:, :, :, span],
            send_sem=halo_send.at[role * KVHEADS + g],
            recv_sem=halo_recv.at[arrival * KVHEADS + g],
            device_id={"tm": lax.rem(tm + hop + n, n)}, device_id_type=MESH)

    firsts, relays, arrivals = [[] for _ in range(KVHEADS)], [], []
    if relayed(plan, x_count, n):
        (_, needed, start), (_, last, start2) = plan
        rest = needed - last
        even, odd = lax.rem(tm, 2) == 0, lax.rem(tm, 2) == 1
        up, down = tm + 2 < n, tm >= 2
        for g in range(KVHEADS):
            firsts[g] += [
                (halo_copy(2, 2, g, kv_ref, frames - last, last, start2, 2), up),
                (halo_copy(3, 3, g, kv_ref, frames - needed, rest, None, -1),
                 jnp.logical_and(odd, up)),
                (halo_copy(0, 0, g, kv_ref, frames - needed, rest, start, 1), even),
                (halo_copy(1, 1, g, kv_ref, frames - last, last, start + rest, 1), even),
            ]
            relays.append([
                (halo_copy(4, 0, g, stash, 0, rest, start, 2), jnp.logical_and(even, up), 3),
                (halo_copy(5, 1, g, kv_win, start2, last, start + rest, -1),
                 jnp.logical_and(odd, down), 2),
            ])
            arrivals.append([
                (0, tm >= 1, rest, start), (1, tm >= 1, last, start + rest),
                (2, jnp.logical_and(even, down), last, start2),
            ])
    else:
        for g in range(KVHEADS):
            for i, (hop, needed, start) in enumerate(plan):
                firsts[g].append((
                    halo_copy(i, i, g, kv_ref, frames - needed, needed, start, hop), tm + hop < n))
            relays.append([])
            arrivals.append([
                (i, tm >= hop, needed, start) for i, (hop, needed, start) in enumerate(plan)])

    def issue(g):
        if g < KVHEADS:
            for copy, mine in firsts[g]:
                pl.when(mine)(copy.start)

    def arrival_of(arrival, g, count, place_at):
        return halo_copy(0, arrival, g, kv_ref, 0, count, place_at, 1)

    def relay(g):
        for copy, mine, arrival in relays[g]:
            @pl.when(mine)
            def _():
                count, place_at = (rest, None) if arrival == 3 else (last, start2)
                arrival_of(arrival, g, count, place_at).wait_recv()
                copy.start()

    def arrive(g):
        for arrival, mine, count, place_at in arrivals[g]:
            pl.when(mine)(arrival_of(arrival, g, count, place_at).wait_recv)

    chunks = ring_chunks(rows, clip, clips)
    steps = n // 2
    started, later = [], []

    def ring_copy(way, step, c):
        start, size, _ = chunks[c]
        owner = index_of(place - step * (1 - 2 * way))
        span = pl.ds(start if isinstance(start, int) else pl.multiple_of(start, TILE_ROWS), size)
        slot = (way * max(steps, 1) + step) * len(chunks) + c
        return pltpu.make_async_remote_copy(
            src_ref=w_ref.at[span] if step == 0 else w_full.at[owner, span],
            dst_ref=w_full.at[owner, span],
            send_sem=ring_send.at[slot], recv_sem=ring_recv.at[slot],
            device_id={"tm": ends[way]}, device_id_type=MESH)

    def goes(way, step, c):
        return n % 2 == 1 or step < steps - 1 or c % 2 == way

    def send_step(way, step, c):
        if step < steps and goes(way, step, c):
            copy = ring_copy(way, step, c)
            copy.start()
            started.append(copy)

    def take(step, c):
        if c < len(chunks):
            for way in range(2):
                if not goes(way, step, c):
                    continue
                ring_copy(way, step, c).wait_recv()
                send_step(way, step + 1, c)
                start, size, over = chunks[c]
                if over:
                    owner = index_of(place - (step + 1) * (1 - 2 * way))
                    span = pl.ds(pl.multiple_of(start, TILE_ROWS), size)
                    slot = (way * steps + step) * len(chunks) + c
                    copy = pltpu.make_async_remote_copy(
                        src_ref=w_full.at[owner, span], dst_ref=w_full.at[owner, span],
                        send_sem=clip_send.at[slot], recv_sem=clip_recv.at[slot],
                        device_id={"clip": 1 - clip}, device_id_type=MESH)
                    copy.start()
                    later.append(copy)

    for c in range(len(chunks)):
        issue(c)
        for way in range(2):
            send_step(way, 0, c)
    for g in range(len(chunks), 3):
        issue(g)

    for hop, needed, start in plan:
        @pl.when(tm < hop)
        def _():
            counts[hop] = jnp.zeros(counts.shape[1:], jnp.int32)
            kv_win[:, start:start + needed] = jnp.zeros(
                (2, needed) + kv_win.shape[2:], kv_win.dtype)

    for hop, copy in count_copies:
        pl.when(tm >= hop)(copy.wait_recv)
    own_copies[0].wait()
    own_copies[1].wait()

    slots = tile * tokens + lax.broadcasted_iota(jnp.int32, (tokens, LANES), 0)
    first_lane = lax.broadcasted_iota(jnp.int32, (tokens, LANES), 1) == 0
    for w in range(LEAD + frames):
        if w >= LEAD:
            row = counts[0, w - LEAD:w - LEAD + 1, :]
        else:
            hop, needed, start = [p for p in plan if p[2] <= w < p[2] + p[1]][0]
            at = frames - needed + w - start
            row = counts[hop, at:at + 1, :]
        bias[w] = jnp.where(
            jnp.logical_and(first_lane, slots >= row), DEAD, 0.0).astype(bias.dtype)

    keys = WINDOW * tokens
    unit_lane = (
        lax.broadcasted_iota(jnp.int32, (groups * tokens, LANES), 1) == 0
    ).astype(jnp.bfloat16)
    ones = jnp.ones((keys, LANES), jnp.bfloat16)
    scale = HEAD_DIM ** (-0.5) * LOG2E
    exchanged = []
    taken = 0
    relay(0)
    for unit in range(KVHEADS * frames):
        g, f = unit // frames, unit % frames
        if f == 0:
            if taken < steps - 1:
                take(taken, 0)
            issue(g + 3)
            arrive(g)
        if f == frames - 1:
            if g + 1 < KVHEADS:
                relay(g + 1)
            if taken < steps - 1:
                take(taken, 1)
                taken += 1
        span = slice(g * HEAD_DIM, (g + 1) * HEAD_DIM)
        k = kv_win[0, f:f + WINDOW, :, span].reshape(keys, HEAD_DIM)
        v = kv_win[1, f:f + WINDOW, :, span].reshape(keys, HEAD_DIM)
        k = jnp.concatenate([k, bias[f:f + WINDOW].reshape(keys, LANES)], axis=1)
        v = jnp.concatenate([v, ones], axis=1)
        q = jnp.concatenate(
            [q_buf[f, :, (g * groups + i) * HEAD_DIM:(g * groups + i + 1) * HEAD_DIM]
             for i in range(groups)], axis=0)
        q = jnp.concatenate([q, unit_lane], axis=1)
        scores = lax.dot_general(q, k, (((1,), (1,)), ((), ())), preferred_element_type=jnp.float32)
        top = jnp.max(scores, axis=-1, keepdims=True)
        weights = jnp.exp2((scores - top) * scale).astype(jnp.bfloat16)
        mixed = jnp.dot(weights, v, preferred_element_type=jnp.float32)
        result = (mixed[:, :HEAD_DIM] / mixed[:, HEAD_DIM:]).astype(jnp.bfloat16)
        for i in range(groups):
            at = (g * groups + i) * HEAD_DIM
            att[f, tile, :, at:at + HEAD_DIM] = result[i * tokens:(i + 1) * tokens]
        if tiles == 2:
            part = att.at[f, tile, :, g * groups * HEAD_DIM:(g + 1) * groups * HEAD_DIM]
            copy = pltpu.make_async_remote_copy(
                src_ref=part, dst_ref=part,
                send_sem=tile_send.at[unit], recv_sem=tile_recv.at[unit],
                device_id={"tile": 1 - tile}, device_id_type=MESH)
            copy.start()
            exchanged.append(copy)
    while taken < steps:
        before_last = list(later)
        take(taken, 0)
        take(taken, 1)
        taken += 1

    columns = w_ref.shape[1]
    same = (
        lax.rem(lax.broadcasted_iota(jnp.int32, (2 * LANES, LANES), 0), LANES) // IDM_DIM
        == lax.broadcasted_iota(jnp.int32, (2 * LANES, LANES), 1) // IDM_DIM
    ).astype(jnp.bfloat16)
    own_copies[2].wait()
    for copy in exchanged:
        copy.wait_recv()

    def projected(f, owners):
        if owners is None:
            return jnp.dot(
                att[f].reshape(tiles * tokens, width), w_full[...].reshape(n * rows, columns),
                preferred_element_type=jnp.float32)
        parts = []
        for owner in owners:
            span = pl.ds(pl.multiple_of(owner * rows, LANES), rows)
            parts.append(jnp.dot(
                att[f, :, :, span].reshape(tiles * tokens, rows), w_full[owner],
                preferred_element_type=jnp.float32))
        return sum(parts)

    first_wave, last_wave = [tm], None
    by_clip = before_last if steps else []
    if rows % LANES == 0 and steps > 1:
        for step in range(steps - 1):
            first_wave += [index_of(place - step - 1), index_of(place + step + 1)]
        last_wave = [index_of(place - steps)]
        if n % 2:
            last_wave.append(index_of(place + steps))
        for copy in by_clip:
            copy.wait_recv()
        for f in range(frames):
            total_ref[f] = projected(f, first_wave)
    else:
        by_clip = []
    for copy in later[len(by_clip):]:
        copy.wait_recv()
    for f in range(frames):
        latent = projected(f, last_wave)
        if last_wave is not None:
            latent = latent + total_ref[f]
        latent = latent.astype(jnp.bfloat16).astype(jnp.float32)
        for c in range(0, columns, LANES):
            value = latent[:, c:c + LANES]
            square = value * value
            high = square.astype(jnp.bfloat16)
            low = (square - high.astype(jnp.float32)).astype(jnp.bfloat16)
            total = jnp.dot(
                jnp.concatenate([high, low], axis=1), same, preferred_element_type=jnp.float32)
            scaled = value * lax.rsqrt(total * (1.0 / IDM_DIM) + 1e-6) * gain_ref[:, c:c + LANES]
            out_ref[f, :, c:c + LANES] = scaled.astype(out_ref.dtype)

    for copy in started + later + exchanged:
        copy.wait_send()
    for hop, copy in count_copies:
        pl.when(tm + hop < n)(copy.wait_send)
    for group in firsts + relays:
        for entry in group:
            pl.when(entry[1])(entry[0].wait_send)


def normed_latent(mesh, queries, keyvals, proj_weight, norm_gain, frame_counts):
    n, clips, tiles = (mesh.shape[a] for a in ("tm", "clip", "tile"))
    frames, tokens, width = queries.shape
    rows, columns = proj_weight.shape
    plan = halo_plan(frames)
    hops = len(plan)
    rest = max(1, plan[0][1] - plan[1][1]) if hops > 1 else 1
    roles = max(6, hops) * KVHEADS
    steps = max(1, n // 2)
    units = frames * KVHEADS
    dma = pltpu.SemaphoreType.DMA
    hbm = pl.BlockSpec(memory_space=pltpu.HBM)
    vmem = pl.BlockSpec(memory_space=pltpu.VMEM)
    bf16 = jnp.bfloat16
    flops = frames * tokens * width * 4 * WINDOW * tokens + 2 * frames * tiles * tokens * width * columns
    return pl.pallas_call(
        functools.partial(latent_kernel, n, clips, tiles, columns_of(mesh)),
        out_shape=jax.ShapeDtypeStruct((frames, tiles * tokens, columns), bf16),
        in_specs=[pl.BlockSpec(memory_space=pltpu.SMEM), hbm, hbm, hbm, vmem],
        out_specs=vmem,
        scratch_shapes=[
            pltpu.VMEM(queries.shape, bf16),
            pltpu.VMEM((2, LEAD + frames) + keyvals.shape[2:], bf16),
            pltpu.VMEM((2, rest) + keyvals.shape[2:], bf16),
            pltpu.VMEM((n, rows, columns), bf16),
            pltpu.VMEM((frames, tiles, tokens, width), bf16),
            pltpu.VMEM((frames, tiles * tokens, columns), jnp.float32),
            pltpu.VMEM((hops + 1, max(8, frames), LANES), jnp.int32),
            pltpu.VMEM((LEAD + frames, tokens, LANES), bf16),
            dma((3,)), dma((roles,)), dma((roles,)), dma((hops,)), dma((hops,)),
            dma((4 * steps,)), dma((4 * steps,)), dma((4 * steps,)), dma((4 * steps,)),
            dma((units,)), dma((units,)),
        ],
        compiler_params=pltpu.CompilerParams(
            collective_id=0, has_side_effects=True, vmem_limit_bytes=60 * 2 ** 20),
        cost_estimate=pl.CostEstimate(
            flops=flops, bytes_accessed=8 * 2 ** 20, transcendentals=0),
    )(frame_counts, queries, keyvals, proj_weight, norm_gain.reshape(1, -1))


def partner_kernel(sources, counts_ref, *refs):
    out_ref = refs[-1]
    frame = pl.program_id(0)
    tokens, columns = out_ref.shape[1:]
    keys = sources * tokens
    slots = lax.broadcasted_iota(jnp.int32, (tokens, LANES), 0)
    live = jnp.concatenate(
        [slots < counts_ref[source, frame] for source in range(sources)], axis=0)
    lower = lax.broadcasted_iota(jnp.int32, (tokens, LANES), 1) < IDM_DIM
    scale = IDM_DIM ** (-0.5) * LOG2E
    for c in range(0, columns, LANES):
        k = jnp.concatenate([ref[0, :, c:c + LANES] for ref in refs[:sources]], axis=0)
        q = refs[0][0, :, c:c + LANES]
        zero = jnp.zeros_like(q)
        q = jnp.concatenate([jnp.where(lower, q, zero), jnp.where(lower, zero, q)], axis=0)
        v = jnp.concatenate(
            [jnp.where(live, k, jnp.zeros_like(k)), live.astype(k.dtype)], axis=1)
        scores = lax.dot_general(q, k, (((1,), (1,)), ((), ())), preferred_element_type=jnp.float32)
        weights = jnp.exp2(scores * scale).astype(jnp.bfloat16)
        mixed = jnp.dot(weights, v, preferred_element_type=jnp.float32)
        result = mixed[:, :LANES] / mixed[:, LANES:]
        out_ref[0, :, c:c + LANES] = jnp.where(
            lower, result[:tokens], result[tokens:]).astype(out_ref.dtype)


def partner_attention(counts, blocks):
    frames, tokens, columns = blocks[0].shape
    spec = pl.BlockSpec((1, tokens, columns), lambda f: (f, 0, 0))
    return pl.pallas_call(
        functools.partial(partner_kernel, len(blocks)),
        out_shape=jax.ShapeDtypeStruct(blocks[0].shape, jnp.bfloat16),
        grid=(frames,),
        in_specs=[pl.BlockSpec(memory_space=pltpu.SMEM)] + [spec] * len(blocks),
        out_specs=spec,
        compiler_params=pltpu.CompilerParams(vmem_limit_bytes=60 * 2 ** 20),
    )(counts, *blocks)


def local(mesh, queries, keyvals, proj_weight, norm_gain, frame_counts):
    normed = normed_latent(mesh, queries, keyvals, proj_weight, norm_gain, frame_counts)
    distance = PARTNER // queries.shape[0]
    blocks, counts = [normed], [frame_counts]
    for steps in (distance, -distance):
        if distance < mesh.shape["tm"]:
            block, count = passed_along((normed, frame_counts), "tm", steps)
            blocks.append(block)
            counts.append(count)
    return partner_attention(jnp.stack(counts), blocks)


def solution(mesh):
    in_specs = (
        P(("clip", "tm"), "tile", None),
        P(None, ("clip", "tm"), "tile", None),
        P("tm", "tile"),
        P("tile"),
        P(("clip", "tm")),
    )
    out_specs = P(("clip", "tm"), None, "tile")
    return jax.shard_map(
        functools.partial(local, mesh), mesh=mesh, in_specs=in_specs, out_specs=out_specs,
        check_vma=False)
```
